32 devices in a mesh: lat: 16 (over z, y, x), obs: 2 (over core).
Axes of the slice: x: 2, y: 2, z: 4, core: 2. Of those that a mesh axis runs over, the one named last changes fastest.
Arguments:
- control: bfloat16 [2, 64, 128, 3072], P(None, 'obs', 'lat'), may hold values from -8 to 8
- zonal_scales: float32 [4], replicated, may hold values from 1.5 to 360, as said below
- zonal_heights: float32 [4], replicated, may hold values from 0.25 to 0.75
- meridional_scales: float32 [4], replicated, may hold values from 0.8 to 180, as said below
- meridional_heights: float32 [4], replicated, may hold values from 0.25 to 0.75
- vertical_map: bfloat16 [2, 64, 64], replicated, may hold values from -0.75 to 0.75
- send_blocks: int32 [16, 2, 2, 2], P('lat', 'obs'), may hold values from 0 to 15
- report_slot: int32 [16, 2, 2048], P('lat', 'obs'), may hold values from 0 to 3
- report_level: int32 [16, 2, 2048], P('lat', 'obs'), may hold values from 0 to 127
- report_corner: int32 [16, 2, 4, 2048], P('lat', 'obs'), may hold values from 0 to 767, as said below
- report_weight: float32 [16, 2, 4, 2048], P('lat', 'obs'), may hold values from 0 to 1, as said below
- innovation: float32 [16, 2, 2048], P('lat', 'obs'), may hold values from -6 to 6
- report_precision: float32 [16, 2, 2048], P('lat', 'obs'), may hold values from 1 to 4
Outputs:
- weighted_departure: float32 [16, 2, 2048], P('lat', 'obs')
- control_gradient: float32 [2, 64, 128, 3072], P(None, 'obs', 'lat')
The draws below stay inside these ranges and needn't reach their ends.
Inputs may be any that keep to these rules, and one draw needn't show every extreme that they name: `report_corner`: the corners of an observation are q, q + 1, q + 192, q + 193 in this order, with q // 192 < 3 and q % 192 < 191. `report_weight`: nonnegative bilinear weights whose four values sum to one, in the corner order of report_corner. `zonal_scales`: positive length scales. `meridional_scales`: positive length scales.
All inputs are finite; a program needn't handle non-finite values.
Results may differ from the reference program's by a relative error of at most 0.009.
Values may be sent and summed in bfloat16 or wider, within the bound.
A program may use at most 128 MiB of HBM per device.

```python
import math
import jax
import jax.numpy as jnp
import numpy as np
from jax import lax

V = 2
L = 64
NX = 3072
REPORTS = 2048
SLOTS = 2
BR = 4
NY = 128
XW = 192
YB = 64
NBLK = 16
N_LAT = 16
N_OBS = 2


def length_scales(key, lows, highs):
    first, second = jax.random.split(key)
    order = jax.random.permutation(first, 4)
    unit = jax.random.uniform(second, (4,), jnp.float32)
    bottom = jnp.log(jnp.array(lows, jnp.float32))
    top = jnp.log(jnp.array(highs, jnp.float32))
    return jnp.exp(bottom + unit * (top - bottom))[order]


def draw_control(key, part):
    key = jax.random.fold_in(key, 21)
    first, second, third = jax.random.split(key, 3)
    wave_number = jax.random.randint(second, (V, L, NY, 1), 40, 71)
    phase = jax.random.uniform(third, (V, L, NY, 1), jnp.float32, 0.0, 2.0 * math.pi)
    cells = jnp.arange(NX, dtype=jnp.int32).reshape(1, 1, 1, NX)
    turn = (wave_number * cells % NX).astype(jnp.float32) * (2.0 * math.pi / NX)
    wave = jnp.cos(turn + phase)
    noise = jnp.clip(jax.random.normal(first, (V, L, NY, NX), jnp.float32), -6.0, 6.0)
    result = noise + wave
    return result.astype(jnp.bfloat16)


def draw_zonal_scales(key, part):
    key = jax.random.fold_in(key, 5)
    return length_scales(key, [2.0, 17.0, 23.0, 90.0], [6.0, 23.0, 30.0, 300.0])


def draw_meridional_scales(key, part):
    key = jax.random.fold_in(key, 9)
    return length_scales(key, [1.0, 3.5, 14.0, 55.0], [2.2, 8.0, 32.0, 150.0])


def draw_report_corner(key, part):
    key = jax.random.fold_in(key, 13)
    first, second = jax.random.split(key)
    row = jax.random.randint(first, (N_LAT, N_OBS, 1, REPORTS), 0, BR - 1)
    cell = jax.random.randint(second, (N_LAT, N_OBS, 1, REPORTS), 0, XW - 1)
    base = row * XW + cell
    base = base.at[:, :, :, 0].set((BR - 2) * XW + XW - 2)
    base = base.at[:, :, :, 1].set(0)
    offsets = jnp.array([0, 1, XW, XW + 1], jnp.int32).reshape(1, 1, 4, 1)
    return (base + offsets).astype(jnp.int32)


def draw_report_weight(key, part):
    key = jax.random.fold_in(key, 17)
    first, second = jax.random.split(key)
    across = jax.random.uniform(first, (N_LAT, N_OBS, 1, REPORTS), jnp.float32)
    upward = jax.random.uniform(second, (N_LAT, N_OBS, 1, REPORTS), jnp.float32)
    return jnp.concatenate([(1.0 - across) * (1.0 - upward), across * (1.0 - upward), (1.0 - across) * upward, across * upward], axis=2)


def touch_ends(values, own_key, smallest, top_value):
    place = [jax.random.randint(jax.random.fold_in(own_key, axis), (), 0, length) for axis, length in enumerate(values.shape)]
    main_axis = values.shape.index(max(values.shape))
    next_to = place[:main_axis] + [(place[main_axis] + 1) % values.shape[main_axis]] + place[main_axis + 1:]
    return values.at[tuple(place)].set(smallest).at[tuple(next_to)].set(top_value)


def block_levels(stream_key, extent, pieces, smallest, high):
    gain = 1.0
    for axis_at, parts in pieces:
        steps = jax.random.uniform(jax.random.fold_in(jax.random.fold_in(stream_key, 6), axis_at), (parts,), jnp.float32, smallest / len(pieces), high / len(pieces))
        gain = gain * jnp.repeat(jnp.exp(steps), extent[axis_at] // parts).reshape((-1,) + (1,) * (len(extent) - 1 - axis_at))
    return gain


def cumulative_ranks(amount, slope):
    portions = [(1 << 20) // math.isqrt(rank ** slope) + 1 for rank in range(1, amount + 1)]
    deviation = 1 + sum(portions) // (1 << 30)
    return np.cumsum(np.array([max(1, weight // deviation) for weight in portions]))


def ranked_ids(stream_key, extent, count, slope):
    table = cumulative_ranks(count, slope)
    lot = jax.random.randint(jax.random.fold_in(stream_key, 1), extent, 0, int(table[count - 1]))
    grade = jnp.searchsorted(jnp.asarray(table, jnp.int32), lot, side="right")
    return jax.random.permutation(jax.random.fold_in(stream_key, 2), count)[grade].astype(jnp.int32)


def centred(own_key, dims, width, most, pieces=(), kind=jnp.bfloat16):
    gain = block_levels(own_key, dims, pieces, -0.22, 0.18) if pieces else 1.0
    values = jax.random.normal(own_key, dims, jnp.float32) * width * gain
    return jnp.minimum(jnp.maximum(values, -most), most).astype(kind)


def setup_inputs(seed: int = 0) -> dict:
    key_list = jax.random.split(jax.random.key(seed), 14)
    control = draw_control(jax.random.fold_in(key_list[13], 71), 0)
    zonal_scales = draw_zonal_scales(jax.random.fold_in(key_list[13], 71), 0)
    zonal_heights = jnp.clip(jax.random.uniform(key_list[2], (4,), jnp.float32, 0.25, 0.75), 0.25, 0.75)
    meridional_scales = draw_meridional_scales(jax.random.fold_in(key_list[13], 71), 0)
    meridional_heights = jnp.clip(jax.random.uniform(key_list[4], (4,), jnp.float32, 0.25, 0.75), 0.25, 0.75)
    vertical_map = centred(key_list[5], (V, L, L), L ** -0.5, 0.75)
    send_blocks = touch_ends(jax.random.randint(key_list[6], (N_LAT, N_OBS, N_OBS, SLOTS), 0, NBLK), jax.random.fold_in(key_list[6], 1), 0, NBLK - 1).astype(jnp.int32)
    report_slot = touch_ends(ranked_ids(key_list[7], (N_LAT, N_OBS, REPORTS), N_OBS * SLOTS, 2), jax.random.fold_in(key_list[7], 3), 0, (N_OBS * SLOTS) - 1).astype(jnp.int32)
    report_level = touch_ends(jax.random.randint(key_list[8], (N_LAT, N_OBS, REPORTS), 0, V * L), jax.random.fold_in(key_list[8], 1), 0, (V * L) - 1).astype(jnp.int32)
    report_corner = draw_report_corner(jax.random.fold_in(key_list[13], 71), 0)
    report_weight = draw_report_weight(jax.random.fold_in(key_list[13], 71), 0)
    innovation = centred(key_list[11], (N_LAT, N_OBS, REPORTS), 1.0, 6.0, ((0, 16), (1, 2)), jnp.float32)
    report_precision = jnp.clip(jnp.exp(math.log(4.0) - 1.3862944 * jax.random.uniform(key_list[12], (N_LAT, N_OBS, REPORTS), jnp.float32) ** block_levels(key_list[12], (N_LAT, N_OBS, REPORTS), ((0, 16), (1, 2)), -0.2, 0.2)), 1.0, 4.0)
    return {"control": control, "zonal_scales": zonal_scales, "zonal_heights": zonal_heights, "meridional_scales": meridional_scales, "meridional_heights": meridional_heights, "vertical_map": vertical_map, "send_blocks": send_blocks, "report_slot": report_slot, "report_level": report_level, "report_corner": report_corner, "report_weight": report_weight, "innovation": innovation, "report_precision": report_precision}


def profile(distance, scales, heights):
    total = jnp.zeros(distance.shape, jnp.float32)
    for member in range(4):
        scale = scales[member]
        total = total + heights[member] * jnp.exp(-distance * distance / (2.0 * scale * scale)) / jnp.sqrt(math.sqrt(math.pi) * scale)
    return total

def reference(control, zonal_scales, zonal_heights, meridional_scales, meridional_heights, vertical_map, send_blocks, report_slot, report_level, report_corner, report_weight, innovation, report_precision):
    offsets = jnp.arange(NX)
    cycle = jnp.minimum(offsets, NX - offsets).astype(jnp.float32)
    kernel = lax.optimization_barrier(profile(cycle, zonal_scales, zonal_heights).astype(jnp.bfloat16)).astype(jnp.float32)
    spectrum = jnp.fft.rfft(kernel)
    places = jnp.arange(NY)
    apart = jnp.abs(places[:, None] - places[None, :]).astype(jnp.float32)
    meridional = profile(apart, meridional_scales, meridional_heights).astype(jnp.bfloat16)

    def along_zonal(plane):
        return jnp.fft.irfft(jnp.fft.rfft(plane.astype(jnp.float32), axis=-1) * spectrum, n=NX, axis=-1)

    def forward_plane(plane):
        smoothed = along_zonal(plane).astype(jnp.bfloat16)
        return jnp.dot(meridional, smoothed, preferred_element_type=jnp.float32).astype(jnp.bfloat16)

    def backward_plane(plane):
        mixed = jnp.dot(meridional.T, plane, preferred_element_type=jnp.float32).astype(jnp.bfloat16)
        return along_zonal(mixed).astype(jnp.float32)
    increments = []
    for variable in range(V):
        lined = lax.map(forward_plane, control[variable])
        mixed = jnp.dot(vertical_map[variable], lined.reshape(L, NY * NX), preferred_element_type=jnp.float32)
        increments.append(mixed.reshape(L, NY, NX))
    increment = jnp.stack(increments)
    lat_ids = jnp.arange(N_LAT).reshape(N_LAT, 1, 1, 1).astype(jnp.int32)
    owner_ids = jnp.arange(N_OBS).reshape(1, N_OBS, 1, 1).astype(jnp.int32)
    slot = report_slot[:, :, None, :]
    anchor = slot // SLOTS
    chosen = send_blocks[lat_ids, anchor, owner_ids, slot % SLOTS]
    code = report_level[:, :, None, :]
    variable_ids = code // L
    level_ids = code % L
    row_ids = anchor * YB + chosen * BR + report_corner // XW
    column_ids = lat_ids * XW + report_corner % XW
    values = increment[variable_ids, level_ids, row_ids, column_ids]
    model_value = lax.optimization_barrier(jnp.sum(report_weight * values, axis=2))
    departure = report_precision * (model_value - innovation)
    pushes = report_weight * departure[:, :, None, :]
    adjoint = jnp.zeros((V, L, NY, NX), jnp.float32).at[variable_ids, level_ids, row_ids, column_ids].add(pushes)
    gradients = []
    for variable in range(V):
        lifted = jnp.dot(vertical_map[variable].astype(jnp.float32).T, adjoint[variable].reshape(L, NY * NX), precision=lax.Precision.HIGHEST)
        lifted = lifted.astype(jnp.bfloat16).reshape(L, NY, NX)
        gradients.append(lax.map(backward_plane, lifted))
    return (departure, jnp.stack(gradients))
```

```python
import functools
import math

import jax
import jax.numpy as jnp
from jax import lax
from jax.experimental import pallas as pl
from jax.experimental.pallas import tpu as pltpu
from jax.sharding import PartitionSpec as P

SLOTS = 2
BR = 4
TILE = 256
F32 = jnp.float32
BF16 = jnp.bfloat16


def coefficients(scales, heights):
    rate = -1.0 / (2.0 * scales * scales)
    gain = heights / jnp.sqrt(math.sqrt(math.pi) * scales)
    return jnp.concatenate([rate, gain]).astype(F32)


def gaussians(distance, coef):
    square = distance * distance
    total = coef[4] * jnp.exp(square * coef[0])
    for member in range(1, 4):
        total = total + coef[4 + member] * jnp.exp(square * coef[member])
    return total


def params(mib=48):
    return pltpu.CompilerParams(vmem_limit_bytes=mib * 1024 * 1024)


def cost(flops, nbytes):
    return pl.CostEstimate(flops=int(flops), bytes_accessed=int(nbytes), transcendentals=0)


def wide_table_kernel(width, coef, out):
    step = 512

    def piece(at, carry):
        start = pl.multiple_of(at * step, step)
        lane = lax.broadcasted_iota(jnp.int32, (TILE, step), 1) + start
        row = lax.broadcasted_iota(jnp.int32, (TILE, step), 0)
        offset = jnp.abs(lane - row)
        distance = jnp.minimum(offset, width - offset).astype(F32)
        value = gaussians(distance, coef).astype(BF16)
        out[:, pl.ds(start, step)] = value
        out[:, pl.ds(start + width, step)] = value
        return carry

    lax.fori_loop(0, width // step, piece, 0)


def tall_table_kernel(width, coef, out):
    step = 512

    def piece(at, carry):
        start = pl.multiple_of(at * step, step)
        row = lax.broadcasted_iota(jnp.int32, (step, TILE), 0) + start
        lane = lax.broadcasted_iota(jnp.int32, (step, TILE), 1)
        offset = jnp.abs(lane - row)
        distance = jnp.minimum(offset, width - offset).astype(F32)
        value = gaussians(distance, coef).astype(BF16)
        out[pl.ds(start, step), :] = value
        out[pl.ds(start + width, step), :] = value
        return carry

    lax.fori_loop(0, width // step, piece, 0)


def table(kernel, shape, width, coef):
    return pl.pallas_call(
        functools.partial(kernel, width),
        out_shape=jax.ShapeDtypeStruct(shape, BF16),
        in_specs=[pl.BlockSpec(memory_space=pltpu.SMEM)],
        out_specs=pl.BlockSpec(memory_space=pltpu.VMEM),
        compiler_params=params(),
        cost_estimate=cost(shape[0] * shape[1] * 30, shape[0] * shape[1] * 2),
    )(coef)


def zonal_forward_kernel(width, control, wide, out, turned):
    at = pl.program_id(0)

    @pl.when(at == 0)
    def _():
        for part in range(width // TILE):
            cells = slice(part * TILE, (part + 1) * TILE)
            turned[cells, :] = control[0, :, cells].T

    start = pl.multiple_of(width - at * TILE, TILE)
    out[...] = jnp.dot(
        wide[:, pl.ds(start, width)], turned[...], preferred_element_type=F32
    ).astype(BF16)


def zonal_forward(control, wide, variable):
    _, rows, width = control.shape
    return pl.pallas_call(
        functools.partial(zonal_forward_kernel, width),
        out_shape=jax.ShapeDtypeStruct((width, rows), BF16),
        grid=(width // TILE,),
        in_specs=[
            pl.BlockSpec((1, rows, width), lambda at: (variable, 0, 0)),
            pl.BlockSpec((TILE, 2 * width), lambda at: (0, 0)),
        ],
        out_specs=pl.BlockSpec((TILE, rows), lambda at: (at, 0)),
        scratch_shapes=[pltpu.VMEM((width, rows), BF16)],
        compiler_params=params(),
        cost_estimate=cost(2 * rows * width * width, 10 * rows * width),
    )(control, wide)


def zonal_backward_kernel(width, lines, tall, *rest):
    out, turned = rest[-2:]
    at = pl.program_id(0)

    @pl.when(at == 0)
    def _():
        for part in range(width // TILE):
            cells = slice(part * TILE, (part + 1) * TILE)
            turned[:, cells] = lines[cells, :].T

    start = pl.multiple_of(width - at * TILE, TILE)
    out[0] = jnp.dot(turned[...], tall[pl.ds(start, width), :], preferred_element_type=F32)


def zonal_backward(lines, tall, variables, variable, gradient):
    width, rows = lines.shape
    operands = [lines, tall]
    in_specs = [
        pl.BlockSpec((width, rows), lambda at: (0, 0)),
        pl.BlockSpec((2 * width, TILE), lambda at: (0, 0)),
    ]
    aliases = {}
    if gradient is not None:
        operands.append(gradient)
        in_specs.append(pl.BlockSpec(memory_space=pl.ANY))
        aliases = {2: 0}
    return pl.pallas_call(
        functools.partial(zonal_backward_kernel, width),
        out_shape=jax.ShapeDtypeStruct((variables, rows, width), F32),
        grid=(width // TILE,),
        in_specs=in_specs,
        out_specs=pl.BlockSpec((1, rows, TILE), lambda at: (variable, 0, at)),
        scratch_shapes=[pltpu.VMEM((rows, width), BF16)],
        input_output_aliases=aliases,
        compiler_params=params(),
        cost_estimate=cost(2 * rows * width * width, 12 * rows * width),
    )(*operands)


def band_matrix(spread, levels, dtype):
    rows, columns = spread.shape
    full = jnp.broadcast_to(spread[None], (levels, rows, columns))
    level = lax.broadcasted_iota(jnp.int32, full.shape, 0)
    lane = lax.broadcasted_iota(jnp.int32, full.shape, 2)
    full = jnp.where(lane % levels == level, full, 0.0)
    return full.reshape(levels * rows, columns).astype(dtype)


def meridional_forward_kernel(levels, owners, lines, spread, out, total):
    at = pl.program_id(0)
    product = jnp.dot(
        lines[0], band_matrix(spread[...], levels, BF16), preferred_element_type=F32
    )

    @pl.when(at == 0)
    def _():
        total[...] = product

    @pl.when(at > 0)
    def _():
        total[...] += product

    @pl.when(at == pl.num_programs(0) - 1)
    def _():
        share = total.shape[1] // owners
        for owner in range(owners):
            out[owner] = total[:, owner * share : (owner + 1) * share].astype(BF16)


def meridional_forward(lines, spread, levels, owners):
    bands, strip, rows = lines.shape
    columns = spread.shape[1]
    band_rows = rows // levels
    return pl.pallas_call(
        functools.partial(meridional_forward_kernel, levels, owners),
        out_shape=jax.ShapeDtypeStruct((owners, strip, columns // owners), BF16),
        grid=(bands,),
        in_specs=[
            pl.BlockSpec((1, strip, rows), lambda at: (at, 0, 0)),
            pl.BlockSpec((band_rows, columns), lambda at: (at, 0)),
        ],
        out_specs=pl.BlockSpec((owners, strip, columns // owners), lambda at: (0, 0, 0)),
        scratch_shapes=[pltpu.VMEM((strip, columns), F32)],
        compiler_params=params(),
        cost_estimate=cost(2 * bands * strip * rows * columns, 2 * bands * strip * rows),
    )(lines, spread)


def meridional_backward_kernel(levels, owners, lifted, spread, out):
    matrix = band_matrix(spread[...], levels, BF16)
    share = matrix.shape[1] // owners
    total = None
    for owner in range(owners):
        part = lax.dot_general(
            lifted[owner],
            matrix[:, owner * share : (owner + 1) * share],
            (((1,), (1,)), ((), ())),
            preferred_element_type=F32,
        )
        total = part if total is None else total + part
    out[0] = total.astype(BF16)


def meridional_backward(lifted, spread, levels, bands):
    owners, strip, share = lifted.shape
    all_rows, columns = spread.shape
    band_rows = all_rows // bands
    rows = levels * band_rows
    return pl.pallas_call(
        functools.partial(meridional_backward_kernel, levels, owners),
        out_shape=jax.ShapeDtypeStruct((bands, strip, rows), BF16),
        grid=(bands,),
        in_specs=[
            pl.BlockSpec((owners, strip, share), lambda at: (0, 0, 0)),
            pl.BlockSpec((band_rows, columns), lambda at: (at, 0)),
        ],
        out_specs=pl.BlockSpec((1, strip, rows), lambda at: (at, 0, 0)),
        compiler_params=params(),
        cost_estimate=cost(2 * bands * strip * rows * columns, 2 * bands * strip * rows),
    )(lifted, spread)


def stencil_kernel(places, weights, out):
    cells = lax.broadcasted_iota(jnp.int32, out.shape, 1)
    value = jnp.zeros(out.shape, F32)
    for corner in range(4):
        hit = cells == places[:, corner : corner + 1]
        value = jnp.where(hit, weights[:, corner : corner + 1], value)
    out[...] = value.astype(BF16)


def stencil(places, weights, points):
    reports = places.shape[0]
    block = min(reports, 256)
    return pl.pallas_call(
        stencil_kernel,
        out_shape=jax.ShapeDtypeStruct((reports, points), BF16),
        grid=(reports // block,),
        in_specs=[
            pl.BlockSpec((block, 4), lambda at: (at, 0)),
            pl.BlockSpec((block, 4), lambda at: (at, 0)),
        ],
        out_specs=pl.BlockSpec((block, points), lambda at: (at, 0)),
        compiler_params=params(),
        cost_estimate=cost(10 * reports * points, 2 * reports * points),
    )(places, weights)


def turned_stencil_kernel(places, weights, out):
    base = pl.program_id(0) * out.shape[0]
    cells = lax.broadcasted_iota(jnp.int32, out.shape, 0) + base
    value = jnp.zeros(out.shape, F32)
    for corner in range(4):
        hit = cells == places[corner : corner + 1, :]
        value = jnp.where(hit, weights[corner : corner + 1, :], value)
    out[...] = value.astype(BF16)


def turned_stencil(places, weights, points):
    reports = places.shape[1]
    block = math.gcd(points, 256)
    return pl.pallas_call(
        turned_stencil_kernel,
        out_shape=jax.ShapeDtypeStruct((points, reports), BF16),
        grid=(points // block,),
        in_specs=[
            pl.BlockSpec((4, reports), lambda at: (0, 0)),
            pl.BlockSpec((4, reports), lambda at: (0, 0)),
        ],
        out_specs=pl.BlockSpec((block, reports), lambda at: (at, 0)),
        compiler_params=params(),
        cost_estimate=cost(10 * reports * points, 2 * reports * points),
    )(places, weights)


def observe_kernel(matrix, field, mapping, innovation, precision, departure, pushes):
    values = jnp.dot(matrix[...], field[...], preferred_element_type=F32)
    mapped = mapping[...]
    model = jnp.sum(values * mapped, axis=1, keepdims=True)
    result = precision[...] * (model - innovation[...])
    departure[...] = result
    pushes[...] = (mapped * result).astype(BF16)


def observe(matrix, field, mapping, innovation, precision):
    reports, points = matrix.shape
    levels = field.shape[1]
    block = min(reports, 256)
    column = pl.BlockSpec((block, 1), lambda at: (at, 0))
    return pl.pallas_call(
        observe_kernel,
        out_shape=(
            jax.ShapeDtypeStruct((reports, 1), F32),
            jax.ShapeDtypeStruct((reports, levels), BF16),
        ),
        grid=(reports // block,),
        in_specs=[
            pl.BlockSpec((block, points), lambda at: (at, 0)),
            pl.BlockSpec((points, levels), lambda at: (0, 0)),
            pl.BlockSpec((block, levels), lambda at: (at, 0)),
            column,
            column,
        ],
        out_specs=(column, pl.BlockSpec((block, levels), lambda at: (at, 0))),
        compiler_params=params(),
        cost_estimate=cost(4 * reports * points * 128, 2 * reports * points),
    )(matrix, field, mapping, innovation, precision)


def spread_kernel(matrix, pushes, out):
    out[...] = jnp.dot(matrix[...], pushes[...], preferred_element_type=F32).astype(BF16)


def spread_reports(matrix, pushes):
    points, reports = matrix.shape
    levels = pushes.shape[1]
    block = math.gcd(points, 768)
    return pl.pallas_call(
        spread_kernel,
        out_shape=jax.ShapeDtypeStruct((points, levels), BF16),
        grid=(points // block,),
        in_specs=[
            pl.BlockSpec((block, reports), lambda at: (at, 0)),
            pl.BlockSpec((reports, levels), lambda at: (0, 0)),
        ],
        out_specs=pl.BlockSpec((block, levels), lambda at: (at, 0)),
        compiler_params=params(),
        cost_estimate=cost(4 * reports * points * 128, 2 * reports * points),
    )(matrix, pushes)


def on_device(
    control,
    zonal_scales,
    zonal_heights,
    meridional_scales,
    meridional_heights,
    vertical_map,
    send_blocks,
    report_slot,
    report_level,
    report_corner,
    report_weight,
    innovation,
    report_precision,
):
    lat_count = lax.axis_size("lat")
    owners = lax.axis_size("obs")
    variables, share, band_rows, width = control.shape
    strip = width // lat_count
    all_rows = band_rows * lat_count
    levels = share * owners
    slots = owners * SLOTS
    kept = slots * BR
    points = strip * kept
    reports = report_slot.shape[-1]

    zonal = coefficients(zonal_scales, zonal_heights)
    wide = table(wide_table_kernel, (TILE, 2 * width), width, zonal)
    fields = control.reshape(variables, share * band_rows, width)
    sent = []
    for variable in range(variables):
        smooth = zonal_forward(fields, wide, variable).reshape(lat_count, strip, -1)
        sent.append(lax.all_to_all(smooth, "lat", split_axis=0, concat_axis=0, tiled=True))

    tall = table(tall_table_kernel, (2 * width, TILE), width, zonal)

    blocks = lax.all_gather(send_blocks.reshape(owners, SLOTS), "obs", axis=0)
    source = jnp.arange(owners)[:, None, None]
    starts = jnp.transpose(source * (all_rows // owners) + blocks * BR, (1, 0, 2))
    rows = starts[..., None] + jnp.arange(BR)
    lanes = jnp.repeat(rows.reshape(-1), share)
    apart = jnp.abs(jnp.arange(all_rows)[:, None] - lanes[None, :]).astype(F32)
    meridional = coefficients(meridional_scales, meridional_heights)
    spread = gaussians(apart, meridional).astype(BF16).astype(F32)

    slot = report_slot.reshape(1, reports)
    code = report_level.reshape(reports)
    corner = report_corner.reshape(4, reports)
    weight = report_weight.reshape(4, reports)
    places = (corner % strip) * kept + slot * BR + corner // strip
    matrix = stencil(places.T, weight.T, points)
    turned = turned_stencil(places, weight, points)
    chosen = (code[:, None] == jnp.arange(variables * levels)[None, :]).astype(BF16)
    innovations = innovation.reshape(reports, 1)
    precisions = report_precision.reshape(reports, 1)

    departures = []
    lines = []
    for variable in range(variables):
        mapping = jnp.dot(
            chosen[:, variable * levels : (variable + 1) * levels],
            vertical_map[variable],
            preferred_element_type=F32,
        )
        mixed = meridional_forward(sent[variable], spread, share, owners)
        taken = lax.all_to_all(mixed, "obs", split_axis=0, concat_axis=0, tiled=True)
        field = taken.reshape(owners, points, share).transpose(1, 0, 2).reshape(points, levels)
        departure, pushes = observe(matrix, field, mapping, innovations, precisions)
        departures.append(departure.reshape(reports))
        adjoint = spread_reports(turned, pushes)
        parts = adjoint.reshape(points, owners, share).transpose(1, 0, 2)
        lifted = lax.all_to_all(
            parts.reshape(owners, strip, kept * share), "obs", split_axis=0, concat_axis=0, tiled=True
        )
        back = meridional_backward(lifted, spread, share, lat_count)
        lines.append(lax.all_to_all(back, "lat", split_axis=0, concat_axis=0, tiled=True))

    gradient = None
    for variable in range(variables):
        gradient = zonal_backward(
            lines[variable].reshape(width, -1), tall, variables, variable, gradient
        )
    departure = departures[0]
    for variable in range(1, variables):
        departure = jnp.where(code >= variable * levels, departures[variable], departure)
    return (departure.reshape(report_slot.shape), gradient.reshape(control.shape))


def solution(mesh):
    in_specs = (
        P(None, "obs", "lat", None),
        P(),
        P(),
        P(),
        P(),
        P(),
        P("lat", "obs", None, None),
        P("lat", "obs", None),
        P("lat", "obs", None),
        P("lat", "obs", None, None),
        P("lat", "obs", None, None),
        P("lat", "obs", None),
        P("lat", "obs", None),
    )
    out_specs = (P("lat", "obs", None), P(None, "obs", "lat", None))
    return jax.shard_map(
        on_device, mesh=mesh, in_specs=in_specs, out_specs=out_specs, check_vma=False
    )
```

```python
import functools
import math

import jax
import jax.numpy as jnp
from jax import lax
from jax.experimental import pallas as pl
from jax.experimental.pallas import tpu as pltpu
from jax.sharding import PartitionSpec as P

SLOTS = 2
BR = 4
TILE = 256
F32 = jnp.float32
BF16 = jnp.bfloat16


def coefficients(scales, heights):
    rate = -1.0 / (2.0 * scales * scales)
    gain = heights / jnp.sqrt(math.sqrt(math.pi) * scales)
    return jnp.concatenate([rate, gain]).astype(F32)


def gaussians(distance, coef):
    square = distance * distance
    total = coef[4] * jnp.exp(square * coef[0])
    for member in range(1, 4):
        total = total + coef[4 + member] * jnp.exp(square * coef[member])
    return total


def params(mib=48):
    return pltpu.CompilerParams(vmem_limit_bytes=mib * 1024 * 1024)


def cost(flops, nbytes):
    return pl.CostEstimate(flops=int(flops), bytes_accessed=int(nbytes), transcendentals=0)


def wide_table_kernel(width, coef, out):
    step = 512

    def piece(at, carry):
        start = pl.multiple_of(at * step, step)
        lane = lax.broadcasted_iota(jnp.int32, (TILE, step), 1) + start
        row = lax.broadcasted_iota(jnp.int32, (TILE, step), 0)
        offset = jnp.abs(lane - row)
        distance = jnp.minimum(offset, width - offset).astype(F32)
        value = gaussians(distance, coef).astype(BF16)
        out[:, pl.ds(start, step)] = value
        out[:, pl.ds(start + width, step)] = value
        return carry

    lax.fori_loop(0, width // step, piece, 0)


def tall_table_kernel(width, coef, out):
    step = 512

    def piece(at, carry):
        start = pl.multiple_of(at * step, step)
        row = lax.broadcasted_iota(jnp.int32, (step, TILE), 0) + start
        lane = lax.broadcasted_iota(jnp.int32, (step, TILE), 1)
        offset = jnp.abs(lane - row)
        distance = jnp.minimum(offset, width - offset).astype(F32)
        value = gaussians(distance, coef).astype(BF16)
        out[pl.ds(start, step), :] = value
        out[pl.ds(start + width, step), :] = value
        return carry

    lax.fori_loop(0, width // step, piece, 0)


def table(kernel, shape, width, coef):
    return pl.pallas_call(
        functools.partial(kernel, width),
        out_shape=jax.ShapeDtypeStruct(shape, BF16),
        in_specs=[pl.BlockSpec(memory_space=pltpu.SMEM)],
        out_specs=pl.BlockSpec(memory_space=pltpu.VMEM),
        compiler_params=params(),
        cost_estimate=cost(shape[0] * shape[1] * 30, shape[0] * shape[1] * 2),
    )(coef)


def zonal_forward_kernel(width, control, wide, out, turned):
    at = pl.program_id(0)

    @pl.when(at == 0)
    def _():
        for part in range(width // TILE):
            cells = slice(part * TILE, (part + 1) * TILE)
            turned[cells, :] = control[0, :, cells].T

    start = pl.multiple_of(width - at * TILE, TILE)
    out[...] = jnp.dot(
        wide[:, pl.ds(start, width)], turned[...], preferred_element_type=F32
    ).astype(BF16)


def zonal_forward(control, wide, variable):
    _, rows, width = control.shape
    return pl.pallas_call(
        functools.partial(zonal_forward_kernel, width),
        out_shape=jax.ShapeDtypeStruct((width, rows), BF16),
        grid=(width // TILE,),
        in_specs=[
            pl.BlockSpec((1, rows, width), lambda at: (variable, 0, 0)),
            pl.BlockSpec((TILE, 2 * width), lambda at: (0, 0)),
        ],
        out_specs=pl.BlockSpec((TILE, rows), lambda at: (at, 0)),
        scratch_shapes=[pltpu.VMEM((width, rows), BF16)],
        compiler_params=params(),
        cost_estimate=cost(2 * rows * width * width, 10 * rows * width),
    )(control, wide)


def zonal_backward_kernel(width, lines, tall, *rest):
    out, turned = rest[-2:]
    at = pl.program_id(0)

    @pl.when(at == 0)
    def _():
        for part in range(width // TILE):
            cells = slice(part * TILE, (part + 1) * TILE)
            turned[:, cells] = lines[cells, :].T

    start = pl.multiple_of(width - at * TILE, TILE)
    out[0] = jnp.dot(turned[...], tall[pl.ds(start, width), :], preferred_element_type=F32)


def zonal_backward(lines, tall, variables, variable, gradient):
    width, rows = lines.shape
    operands = [lines, tall]
    in_specs = [
        pl.BlockSpec((width, rows), lambda at: (0, 0)),
        pl.BlockSpec((2 * width, TILE), lambda at: (0, 0)),
    ]
    aliases = {}
    if gradient is not None:
        operands.append(gradient)
        in_specs.append(pl.BlockSpec(memory_space=pl.ANY))
        aliases = {2: 0}
    return pl.pallas_call(
        functools.partial(zonal_backward_kernel, width),
        out_shape=jax.ShapeDtypeStruct((variables, rows, width), F32),
        grid=(width // TILE,),
        in_specs=in_specs,
        out_specs=pl.BlockSpec((1, rows, TILE), lambda at: (variable, 0, at)),
        scratch_shapes=[pltpu.VMEM((rows, width), BF16)],
        input_output_aliases=aliases,
        compiler_params=params(),
        cost_estimate=cost(2 * rows * width * width, 12 * rows * width),
    )(*operands)


def band_kernel(levels, spread, out):
    rows, columns = spread.shape
    full = jnp.broadcast_to(spread[...][None], (levels, rows, columns))
    level = lax.broadcasted_iota(jnp.int32, full.shape, 0)
    lane = lax.broadcasted_iota(jnp.int32, (1, 1, columns), 2) % levels
    full = jnp.where(lane == level, full, 0.0)
    out[0] = full.reshape(levels * rows, columns).astype(BF16)


def band_matrices(spread, levels, bands):
    all_rows, columns = spread.shape
    band_rows = all_rows // bands
    rows = levels * band_rows
    return pl.pallas_call(
        functools.partial(band_kernel, levels),
        out_shape=jax.ShapeDtypeStruct((bands, rows, columns), BF16),
        grid=(bands,),
        in_specs=[pl.BlockSpec((band_rows, columns), lambda at: (at, 0))],
        out_specs=pl.BlockSpec((1, rows, columns), lambda at: (at, 0, 0)),
        compiler_params=params(),
        cost_estimate=cost(10 * bands * rows * columns, 2 * bands * rows * columns),
    )(spread)


def meridional_forward_kernel(lines, matrix, out, total):
    at = pl.program_id(0)
    product = jnp.dot(lines[0], matrix[0], preferred_element_type=F32)

    @pl.when(at == 0)
    def _():
        total[...] = product

    @pl.when(at > 0)
    def _():
        total[...] += product

    @pl.when(at == pl.num_programs(0) - 1)
    def _():
        owners, _, share = out.shape
        for owner in range(owners):
            out[owner] = total[:, owner * share : (owner + 1) * share].astype(BF16)


def meridional_forward(lines, matrices, owners):
    bands, strip, rows = lines.shape
    columns = matrices.shape[2]
    return pl.pallas_call(
        meridional_forward_kernel,
        out_shape=jax.ShapeDtypeStruct((owners, strip, columns // owners), BF16),
        grid=(bands,),
        in_specs=[
            pl.BlockSpec((1, strip, rows), lambda at: (at, 0, 0)),
            pl.BlockSpec((1, rows, columns), lambda at: (at, 0, 0)),
        ],
        out_specs=pl.BlockSpec((owners, strip, columns // owners), lambda at: (0, 0, 0)),
        scratch_shapes=[pltpu.VMEM((strip, columns), F32)],
        compiler_params=params(),
        cost_estimate=cost(2 * bands * strip * rows * columns, 2 * bands * strip * rows),
    )(lines, matrices)


def meridional_backward_kernel(own, other, matrix, out):
    share = own.shape[1]
    transposed = (((1,), (1,)), ((), ()))
    total = lax.dot_general(
        own[...], matrix[0, :, :share], transposed, preferred_element_type=F32
    ) + lax.dot_general(other[...], matrix[0, :, share:], transposed, preferred_element_type=F32)
    out[0] = total.astype(BF16)


def meridional_backward(own, other, matrices):
    bands, rows, columns = matrices.shape
    strip, share = own.shape
    half = pl.BlockSpec((strip, share), lambda at: (0, 0))
    return pl.pallas_call(
        meridional_backward_kernel,
        out_shape=jax.ShapeDtypeStruct((bands, strip, rows), BF16),
        grid=(bands,),
        in_specs=[half, half, pl.BlockSpec((1, rows, columns), lambda at: (at, 0, 0))],
        out_specs=pl.BlockSpec((1, strip, rows), lambda at: (at, 0, 0)),
        compiler_params=params(),
        cost_estimate=cost(2 * bands * strip * rows * columns, 2 * bands * strip * rows),
    )(own, other, matrices)


def reports_kernel(variable, share, own, other, ids, numbers, cells, weights, maps, departure, lifted, total):
    at = pl.program_id(0)
    strip, columns = own.shape
    block = ids.shape[0]
    levels = maps.shape[2]
    across = lax.broadcasted_iota(jnp.int32, (block, strip), 1)
    cell = ids[:, 0:1]
    down = lax.broadcasted_iota(jnp.int32, (strip, block), 0)
    place = cells[...]
    sides = []
    turned = []
    for side in range(2):
        value = jnp.where(across == cell, numbers[:, 2 * side : 2 * side + 1], 0.0)
        value = jnp.where(across == cell + 1, numbers[:, 2 * side + 1 : 2 * side + 2], value)
        sides.append(value.astype(BF16))
        value = jnp.where(down == place, weights[2 * side : 2 * side + 1, :], 0.0)
        value = jnp.where(down == place + 1, weights[2 * side + 1 : 2 * side + 2, :], value)
        turned.append(value.astype(BF16))
    level = ids[:, 2:3] - variable * levels
    chosen = jnp.where(lax.broadcasted_iota(jnp.int32, (block, levels), 1) == level, 1.0, 0.0)
    chosen = chosen.astype(BF16)
    lane = lax.broadcasted_iota(jnp.int32, (block, columns), 1) // share
    hits = [lane == ids[:, 1:2], lane == ids[:, 1:2] + 1]
    fields = (own, other)
    model = jnp.zeros((block, 1), F32)
    kept = []
    for half in range(2):
        mapped = jnp.dot(chosen, maps[0, half], preferred_element_type=F32)
        found = jnp.zeros((block, columns), F32)
        for side in range(2):
            picked = jnp.where(hits[side], mapped, 0.0)
            kept.append(picked)
            values = jnp.dot(sides[side], fields[half][...], preferred_element_type=F32)
            found = found + values * picked
        model = model + jnp.sum(found, axis=1, keepdims=True)
    result = numbers[:, 5:6] * (model - numbers[:, 4:5])
    departure[...] = jnp.broadcast_to(result, (block, 128)).T[0:1, :]
    for half in range(2):
        product = jnp.zeros((strip, columns), F32)
        for side in range(2):
            pushes = (kept[2 * half + side] * result).astype(BF16)
            product = product + jnp.dot(turned[side], pushes, preferred_element_type=F32)

        @pl.when(at == 0)
        def _():
            total[half] = product

        @pl.when(at > 0)
        def _():
            total[half] += product

    @pl.when(at == pl.num_programs(0) - 1)
    def _():
        lifted[...] = total[...].astype(BF16)


def at_reports(variable, share, own, other, ids, numbers, cells, weights, maps):
    strip, columns = own.shape
    reports = ids.shape[0]
    block = math.gcd(reports, 256)
    half = pl.BlockSpec((strip, columns), lambda at: (0, 0))
    return pl.pallas_call(
        functools.partial(reports_kernel, variable, share),
        out_shape=(
            jax.ShapeDtypeStruct((1, reports), F32),
            jax.ShapeDtypeStruct((2, strip, columns), BF16),
        ),
        grid=(reports // block,),
        in_specs=[
            half,
            half,
            pl.BlockSpec((block, ids.shape[1]), lambda at: (at, 0)),
            pl.BlockSpec((block, numbers.shape[1]), lambda at: (at, 0)),
            pl.BlockSpec((1, block), lambda at: (0, at)),
            pl.BlockSpec((4, block), lambda at: (0, at)),
            pl.BlockSpec((1,) + maps.shape[1:], lambda at: (variable, 0, 0, 0)),
        ],
        out_specs=(
            pl.BlockSpec((1, block), lambda at: (0, at)),
            pl.BlockSpec((2, strip, columns), lambda at: (0, 0, 0)),
        ),
        scratch_shapes=[pltpu.VMEM((2, strip, columns), F32)],
        compiler_params=params(),
        cost_estimate=cost(16 * reports * 256 * columns, 4 * reports * 128),
    )(own, other, ids, numbers, cells, weights, maps)


def on_device(
    control,
    zonal_scales,
    zonal_heights,
    meridional_scales,
    meridional_heights,
    vertical_map,
    send_blocks,
    report_slot,
    report_level,
    report_corner,
    report_weight,
    innovation,
    report_precision,
):
    lat_count = lax.axis_size("lat")
    owners = lax.axis_size("obs")
    variables, share, band_rows, width = control.shape
    strip = width // lat_count
    all_rows = band_rows * lat_count
    levels = share * owners
    slots = owners * SLOTS
    kept = slots * BR
    points = strip * kept
    reports = report_slot.shape[-1]

    zonal = coefficients(zonal_scales, zonal_heights)
    wide = table(wide_table_kernel, (TILE, 2 * width), width, zonal)
    fields = control.reshape(variables, share * band_rows, width)
    sent = []
    for variable in range(variables):
        smooth = zonal_forward(fields, wide, variable).reshape(lat_count, strip, -1)
        sent.append(lax.all_to_all(smooth, "lat", split_axis=0, concat_axis=0, tiled=True))

    tall = table(tall_table_kernel, (2 * width, TILE), width, zonal)

    me = lax.axis_index("obs")
    partner = [(0, 1), (1, 0)]
    blocks = lax.all_gather(send_blocks.reshape(owners, SLOTS), "obs", axis=0)
    source = jnp.arange(owners)[:, None, None]
    starts = jnp.transpose(source * (all_rows // owners) + blocks * BR, (1, 0, 2))
    starts = jnp.where(me == 0, starts, starts[::-1])
    rows = starts[..., None] + jnp.arange(BR)
    lanes = jnp.repeat(rows.reshape(-1), share)
    apart = jnp.abs(jnp.arange(all_rows)[:, None] - lanes[None, :]).astype(F32)
    meridional = coefficients(meridional_scales, meridional_heights)
    spread = gaussians(apart, meridional).astype(BF16).astype(F32)
    matrices = band_matrices(spread, share, lat_count)

    slot = report_slot.reshape(1, reports)
    code = report_level.reshape(1, reports)
    first = report_corner.reshape(4, reports)[0:1]
    weight = report_weight.reshape(4, reports)
    cells = first % strip
    ids = jnp.concatenate([cells, slot * BR + first // strip, code], axis=0).T
    numbers = jnp.concatenate(
        [weight, innovation.reshape(1, reports), report_precision.reshape(1, reports)], axis=0
    ).T
    maps = vertical_map.reshape(variables, levels, owners, share).transpose(0, 2, 1, 3)
    maps = jnp.where(me == 0, maps, maps[:, ::-1])
    maps = jnp.tile(maps, (1, 1, 1, kept))

    departures = []
    lines = []
    for variable in range(variables):
        mixed = meridional_forward(sent[variable], matrices, owners)
        theirs = lax.ppermute(mixed[1], "obs", partner)
        departure, lifted = at_reports(
            variable, share, mixed[0], theirs, ids, numbers, cells, weight, maps
        )
        departures.append(departure)
        theirs = lax.ppermute(lifted[1], "obs", partner)
        back = meridional_backward(lifted[0], theirs, matrices)
        lines.append(lax.all_to_all(back, "lat", split_axis=0, concat_axis=0, tiled=True))

    gradient = None
    for variable in range(variables):
        gradient = zonal_backward(
            lines[variable].reshape(width, -1), tall, variables, variable, gradient
        )
    departure = departures[0]
    for variable in range(1, variables):
        departure = jnp.where(code >= variable * levels, departures[variable], departure)
    return (departure.reshape(report_slot.shape), gradient.reshape(control.shape))


def solution(mesh):
    in_specs = (
        P(None, "obs", "lat", None),
        P(),
        P(),
        P(),
        P(),
        P(),
        P("lat", "obs", None, None),
        P("lat", "obs", None),
        P("lat", "obs", None),
        P("lat", "obs", None, None),
        P("lat", "obs", None, None),
        P("lat", "obs", None),
        P("lat", "obs", None),
    )
    out_specs = (P("lat", "obs", None), P(None, "obs", "lat", None))
    return jax.shard_map(
        on_device, mesh=mesh, in_specs=in_specs, out_specs=out_specs, check_vma=False
    )
```

```python
import functools
import math

import jax
import jax.numpy as jnp
from jax import lax
from jax.experimental import pallas as pl
from jax.experimental.pallas import tpu as pltpu
from jax.sharding import PartitionSpec as P

SLOTS = 2
BR = 4
TILE = 256
F32 = jnp.float32
BF16 = jnp.bfloat16


def coefficients(scales, heights):
    rate = -1.0 / (2.0 * scales * scales)
    gain = heights / jnp.sqrt(math.sqrt(math.pi) * scales)
    return jnp.concatenate([rate, gain]).astype(F32)


def gaussians(distance, coef):
    square = distance * distance
    total = coef[4] * jnp.exp(square * coef[0])
    for member in range(1, 4):
        total = total + coef[4 + member] * jnp.exp(square * coef[member])
    return total


def params(mib=48):
    return pltpu.CompilerParams(vmem_limit_bytes=mib * 1024 * 1024)


def cost(flops, nbytes):
    return pl.CostEstimate(flops=int(flops), bytes_accessed=int(nbytes), transcendentals=0)


def wide_table_kernel(width, coef, out):
    step = 512

    def piece(at, carry):
        start = pl.multiple_of(at * step, step)
        lane = lax.broadcasted_iota(jnp.int32, (TILE, step), 1) + start
        row = lax.broadcasted_iota(jnp.int32, (TILE, step), 0)
        offset = jnp.abs(lane - row)
        distance = jnp.minimum(offset, width - offset).astype(F32)
        value = gaussians(distance, coef).astype(BF16)
        out[:, pl.ds(start, step)] = value
        out[:, pl.ds(start + width, step)] = value
        return carry

    lax.fori_loop(0, width // step, piece, 0)


def tall_table_kernel(width, coef, out):
    step = 512

    def piece(at, carry):
        start = pl.multiple_of(at * step, step)
        row = lax.broadcasted_iota(jnp.int32, (step, TILE), 0) + start
        lane = lax.broadcasted_iota(jnp.int32, (step, TILE), 1)
        offset = jnp.abs(lane - row)
        distance = jnp.minimum(offset, width - offset).astype(F32)
        value = gaussians(distance, coef).astype(BF16)
        out[pl.ds(start, step), :] = value
        out[pl.ds(start + width, step), :] = value
        return carry

    lax.fori_loop(0, width // step, piece, 0)


def table(kernel, shape, width, coef):
    return pl.pallas_call(
        functools.partial(kernel, width),
        out_shape=jax.ShapeDtypeStruct(shape, BF16),
        in_specs=[pl.BlockSpec(memory_space=pltpu.SMEM)],
        out_specs=pl.BlockSpec(memory_space=pltpu.VMEM),
        compiler_params=params(),
        cost_estimate=cost(shape[0] * shape[1] * 30, shape[0] * shape[1] * 2),
    )(coef)


def zonal_forward_kernel(width, control, wide, out, turned):
    at = pl.program_id(0)

    @pl.when(at == 0)
    def _():
        for part in range(width // TILE):
            cells = slice(part * TILE, (part + 1) * TILE)
            turned[cells, :] = control[0, :, cells].T

    start = pl.multiple_of(width - at * TILE, TILE)
    out[...] = jnp.dot(
        wide[:, pl.ds(start, width)], turned[...], preferred_element_type=F32
    ).astype(BF16)


def zonal_forward(control, wide, variable):
    _, rows, width = control.shape
    return pl.pallas_call(
        functools.partial(zonal_forward_kernel, width),
        out_shape=jax.ShapeDtypeStruct((width, rows), BF16),
        grid=(width // TILE,),
        in_specs=[
            pl.BlockSpec((1, rows, width), lambda at: (variable, 0, 0)),
            pl.BlockSpec((TILE, 2 * width), lambda at: (0, 0)),
        ],
        out_specs=pl.BlockSpec((TILE, rows), lambda at: (at, 0)),
        scratch_shapes=[pltpu.VMEM((width, rows), BF16)],
        compiler_params=params(),
        cost_estimate=cost(2 * rows * width * width, 10 * rows * width),
    )(control, wide)


def zonal_backward_kernel(width, lines, tall, *rest):
    out, turned = rest[-2:]
    at = pl.program_id(0)

    @pl.when(at == 0)
    def _():
        for part in range(width // TILE):
            cells = slice(part * TILE, (part + 1) * TILE)
            turned[:, cells] = lines[cells, :].T

    start = pl.multiple_of(width - at * TILE, TILE)
    out[0] = jnp.dot(turned[...], tall[pl.ds(start, width), :], preferred_element_type=F32)


def zonal_backward(lines, tall, variables, variable, gradient):
    width, rows = lines.shape
    operands = [lines, tall]
    in_specs = [
        pl.BlockSpec((width, rows), lambda at: (0, 0)),
        pl.BlockSpec((2 * width, TILE), lambda at: (0, 0)),
    ]
    aliases = {}
    if gradient is not None:
        operands.append(gradient)
        in_specs.append(pl.BlockSpec(memory_space=pl.ANY))
        aliases = {2: 0}
    return pl.pallas_call(
        functools.partial(zonal_backward_kernel, width),
        out_shape=jax.ShapeDtypeStruct((variables, rows, width), F32),
        grid=(width // TILE,),
        in_specs=in_specs,
        out_specs=pl.BlockSpec((1, rows, TILE), lambda at: (variable, 0, at)),
        scratch_shapes=[pltpu.VMEM((rows, width), BF16)],
        input_output_aliases=aliases,
        compiler_params=params(),
        cost_estimate=cost(2 * rows * width * width, 12 * rows * width),
    )(*operands)


def band_kernel(group, coef, lanes, out):
    pair, band_rows = 2, out.shape[1] // (2 * group)
    columns = out.shape[2]
    base = pl.program_id(0) * pair * band_rows
    row = lax.broadcasted_iota(jnp.int32, (pair * band_rows, columns), 0) + base
    apart = jnp.abs(row - lanes[...]).astype(F32)
    value = gaussians(apart, coef).reshape(pair, 1, band_rows, columns)
    full = jnp.broadcast_to(value, (pair, group, band_rows, columns))
    level = lax.broadcasted_iota(jnp.int32, full.shape, 1)
    lane = lax.broadcasted_iota(jnp.int32, (1, 1, 1, columns), 3) % group
    full = jnp.where(lane == level, full, 0.0)
    out[0] = full.reshape(pair * group * band_rows, columns).astype(BF16)


def band_matrices(coef, lanes, group, band_rows, bands):
    columns = lanes.shape[1]
    rows = 2 * group * band_rows
    return pl.pallas_call(
        functools.partial(band_kernel, group),
        out_shape=jax.ShapeDtypeStruct((bands // 2, rows, columns), BF16),
        grid=(bands // 2,),
        in_specs=[
            pl.BlockSpec(memory_space=pltpu.SMEM),
            pl.BlockSpec((1, columns), lambda at: (0, 0)),
        ],
        out_specs=pl.BlockSpec((1, rows, columns), lambda at: (at, 0, 0)),
        compiler_params=params(),
        cost_estimate=cost(5 * bands * rows * columns, bands * rows * columns),
    )(coef, lanes)


def meridional_forward_kernel(lines, matrix, out, total):
    at = pl.program_id(0)
    groups, strip, columns = total.shape
    part = lines.shape[2] // groups
    owners, share = out.shape[0], columns // out.shape[0]
    for group in range(groups):
        cells = slice(group * part, (group + 1) * part)
        both = jnp.concatenate([lines[0, :, cells], lines[1, :, cells]], axis=1)
        product = jnp.dot(both, matrix[0], preferred_element_type=F32)

        @pl.when(at == 0)
        def _():
            total[group] = product

        @pl.when(at > 0)
        def _():
            total[group] += product

    @pl.when(at == pl.num_programs(0) - 1)
    def _():
        for owner in range(owners):
            for group in range(groups):
                out[owner, :, group * share : (group + 1) * share] = total[
                    group, :, owner * share : (owner + 1) * share
                ].astype(BF16)


def meridional_forward(lines, matrices, owners, groups):
    bands, strip, rows = lines.shape
    pairs, depth, columns = matrices.shape
    return pl.pallas_call(
        meridional_forward_kernel,
        out_shape=jax.ShapeDtypeStruct((owners, strip, groups * columns // owners), BF16),
        grid=(pairs,),
        in_specs=[
            pl.BlockSpec((2, strip, rows), lambda at: (at, 0, 0)),
            pl.BlockSpec((1, depth, columns), lambda at: (at, 0, 0)),
        ],
        out_specs=pl.BlockSpec(
            (owners, strip, groups * columns // owners), lambda at: (0, 0, 0)
        ),
        scratch_shapes=[pltpu.VMEM((groups, strip, columns), F32)],
        compiler_params=params(),
        cost_estimate=cost(2 * bands * strip * rows * columns, 2 * bands * strip * rows),
    )(lines, matrices)


def meridional_backward_kernel(groups, own, other, matrix, out):
    share = own.shape[1] // groups
    part = out.shape[2] // groups
    for group in range(groups):
        cells = slice(group * share, (group + 1) * share)
        both = jnp.concatenate([own[:, cells], other[:, cells]], axis=1)
        product = lax.dot_general(
            both, matrix[0], (((1,), (1,)), ((), ())), preferred_element_type=F32
        ).astype(BF16)
        for band in range(2):
            out[band, :, group * part : (group + 1) * part] = product[
                :, band * part : (band + 1) * part
            ]


def meridional_backward(own, other, matrices, groups):
    pairs, depth, columns = matrices.shape
    strip, share = own.shape
    rows = depth * groups // 2
    half = pl.BlockSpec((strip, share), lambda at: (0, 0))
    return pl.pallas_call(
        functools.partial(meridional_backward_kernel, groups),
        out_shape=jax.ShapeDtypeStruct((2 * pairs, strip, rows), BF16),
        grid=(pairs,),
        in_specs=[half, half, pl.BlockSpec((1, depth, columns), lambda at: (at, 0, 0))],
        out_specs=pl.BlockSpec((2, strip, rows), lambda at: (at, 0, 0)),
        compiler_params=params(),
        cost_estimate=cost(4 * pairs * strip * rows * columns, 4 * pairs * strip * rows),
    )(own, other, matrices)


def reports_kernel(variable, group, kept_rows, own, other, ids, numbers, cells, weights, maps, departure, lifted, total):
    at = pl.program_id(0)
    strip, columns = own.shape
    block = ids.shape[0]
    levels = maps.shape[2]
    across = lax.broadcasted_iota(jnp.int32, (block, strip), 1)
    cell = ids[:, 0:1]
    down = lax.broadcasted_iota(jnp.int32, (strip, block), 0)
    place = cells[...]
    sides = []
    turned = []
    for side in range(2):
        value = jnp.where(across == cell, numbers[:, 2 * side : 2 * side + 1], 0.0)
        value = jnp.where(across == cell + 1, numbers[:, 2 * side + 1 : 2 * side + 2], value)
        sides.append(value.astype(BF16))
        value = jnp.where(down == place, weights[2 * side : 2 * side + 1, :], 0.0)
        value = jnp.where(down == place + 1, weights[2 * side + 1 : 2 * side + 2, :], value)
        turned.append(value.astype(BF16))
    level = ids[:, 2:3] - variable * levels
    chosen = jnp.where(lax.broadcasted_iota(jnp.int32, (block, levels), 1) == level, 1.0, 0.0)
    chosen = chosen.astype(BF16)
    lane = lax.broadcasted_iota(jnp.int32, (block, columns), 1) // group % kept_rows
    hits = [lane == ids[:, 1:2], lane == ids[:, 1:2] + 1]
    fields = (own, other)
    model = jnp.zeros((block, 1), F32)
    kept = []
    for half in range(2):
        mapped = jnp.dot(chosen, maps[0, half], preferred_element_type=F32)
        found = jnp.zeros((block, columns), F32)
        for side in range(2):
            picked = jnp.where(hits[side], mapped, 0.0)
            kept.append(picked)
            values = jnp.dot(sides[side], fields[half][...], preferred_element_type=F32)
            found = found + values * picked
        model = model + jnp.sum(found, axis=1, keepdims=True)
    result = numbers[:, 5:6] * (model - numbers[:, 4:5])
    both = jnp.concatenate(turned, axis=1)
    departure[...] = jnp.broadcast_to(result, (block, 128)).T[0:1, :]
    for half in range(2):
        pushes = [(kept[2 * half + side] * result).astype(BF16) for side in range(2)]
        product = jnp.dot(both, jnp.concatenate(pushes, axis=0), preferred_element_type=F32)

        @pl.when(at == 0)
        def _():
            total[half] = product

        @pl.when(at > 0)
        def _():
            total[half] += product

    @pl.when(at == pl.num_programs(0) - 1)
    def _():
        lifted[...] = total[...].astype(BF16)


def at_reports(variable, group, kept_rows, own, other, ids, numbers, cells, weights, maps):
    strip, columns = own.shape
    reports = ids.shape[0]
    block = math.gcd(reports, 256)
    half = pl.BlockSpec((strip, columns), lambda at: (0, 0))
    return pl.pallas_call(
        functools.partial(reports_kernel, variable, group, kept_rows),
        out_shape=(
            jax.ShapeDtypeStruct((1, reports), F32),
            jax.ShapeDtypeStruct((2, strip, columns), BF16),
        ),
        grid=(reports // block,),
        in_specs=[
            half,
            half,
            pl.BlockSpec((block, ids.shape[1]), lambda at: (at, 0)),
            pl.BlockSpec((block, numbers.shape[1]), lambda at: (at, 0)),
            pl.BlockSpec((1, block), lambda at: (0, at)),
            pl.BlockSpec((4, block), lambda at: (0, at)),
            pl.BlockSpec((1,) + maps.shape[1:], lambda at: (variable, 0, 0, 0)),
        ],
        out_specs=(
            pl.BlockSpec((1, block), lambda at: (0, at)),
            pl.BlockSpec((2, strip, columns), lambda at: (0, 0, 0)),
        ),
        scratch_shapes=[pltpu.VMEM((2, strip, columns), F32)],
        compiler_params=params(),
        cost_estimate=cost(16 * reports * 256 * columns, 4 * reports * 128),
    )(own, other, ids, numbers, cells, weights, maps)


def on_device(
    control,
    zonal_scales,
    zonal_heights,
    meridional_scales,
    meridional_heights,
    vertical_map,
    send_blocks,
    report_slot,
    report_level,
    report_corner,
    report_weight,
    innovation,
    report_precision,
):
    lat_count = lax.axis_size("lat")
    owners = lax.axis_size("obs")
    variables, share, band_rows, width = control.shape
    strip = width // lat_count
    all_rows = band_rows * lat_count
    levels = share * owners
    slots = owners * SLOTS
    kept = slots * BR
    points = strip * kept
    reports = report_slot.shape[-1]

    zonal = coefficients(zonal_scales, zonal_heights)
    wide = table(wide_table_kernel, (TILE, 2 * width), width, zonal)
    fields = control.reshape(variables, share * band_rows, width)
    smooth = [
        zonal_forward(fields, wide, variable).reshape(lat_count, strip, -1)
        for variable in range(variables)
    ]

    group = 128 // band_rows
    groups = share // group
    me = lax.axis_index("obs")
    partner = [(0, 1), (1, 0)]
    blocks = lax.all_gather(send_blocks.reshape(owners, SLOTS), "obs", axis=0)
    source = jnp.arange(owners)[:, None, None]
    starts = jnp.transpose(source * (all_rows // owners) + blocks * BR, (1, 0, 2))
    starts = jnp.where(me == 0, starts, starts[::-1])
    rows = starts[..., None] + jnp.arange(BR)
    lanes = jnp.repeat(rows.reshape(-1), group).reshape(1, -1).astype(jnp.int32)
    meridional = coefficients(meridional_scales, meridional_heights)
    matrices = band_matrices(meridional, lanes, group, band_rows, lat_count)

    slot = report_slot.reshape(1, reports)
    code = report_level.reshape(1, reports)
    first = report_corner.reshape(4, reports)[0:1]
    weight = report_weight.reshape(4, reports)
    cells = first % strip
    ids = jnp.concatenate([cells, slot * BR + first // strip, code], axis=0).T
    numbers = jnp.concatenate(
        [weight, innovation.reshape(1, reports), report_precision.reshape(1, reports)], axis=0
    ).T
    maps = vertical_map.reshape(variables, levels, owners, groups, 1, group)
    maps = maps.transpose(0, 2, 1, 3, 4, 5)
    maps = jnp.where(me == 0, maps, maps[:, ::-1])
    maps = jnp.broadcast_to(maps, (variables, owners, levels, groups, kept, group))
    maps = maps.reshape(variables, owners, levels, groups * kept * group)
    tall = table(tall_table_kernel, (2 * width, TILE), width, zonal)

    last, matrices, ids, numbers, cells, maps, tall = lax.optimization_barrier(
        (smooth[-1], matrices, ids, numbers, cells, maps, tall)
    )
    smooth[-1] = last
    sent = [
        lax.all_to_all(part, "lat", split_axis=0, concat_axis=0, tiled=True) for part in smooth
    ]

    departures = []
    lines = []
    for variable in range(variables):
        mixed = meridional_forward(sent[variable], matrices, owners, groups)
        theirs = lax.ppermute(mixed[1], "obs", partner)
        departure, lifted = at_reports(
            variable, group, kept, mixed[0], theirs, ids, numbers, cells, weight, maps
        )
        departures.append(departure)
        theirs = lax.ppermute(lifted[1], "obs", partner)
        back = meridional_backward(lifted[0], theirs, matrices, groups)
        lines.append(lax.all_to_all(back, "lat", split_axis=0, concat_axis=0, tiled=True))

    gradient = None
    for variable in range(variables):
        gradient = zonal_backward(
            lines[variable].reshape(width, -1), tall, variables, variable, gradient
        )
    departure = departures[0]
    for variable in range(1, variables):
        departure = jnp.where(code >= variable * levels, departures[variable], departure)
    return (departure.reshape(report_slot.shape), gradient.reshape(control.shape))


def solution(mesh):
    in_specs = (
        P(None, "obs", "lat", None),
        P(),
        P(),
        P(),
        P(),
        P(),
        P("lat", "obs", None, None),
        P("lat", "obs", None),
        P("lat", "obs", None),
        P("lat", "obs", None, None),
        P("lat", "obs", None, None),
        P("lat", "obs", None),
        P("lat", "obs", None),
    )
    out_specs = (P("lat", "obs", None), P(None, "obs", "lat", None))
    return jax.shard_map(
        on_device, mesh=mesh, in_specs=in_specs, out_specs=out_specs, check_vma=False
    )
```

```python
import functools
import math

import jax
import jax.numpy as jnp
from jax import lax
from jax.experimental import pallas as pl
from jax.experimental.pallas import tpu as pltpu
from jax.sharding import PartitionSpec as P

SLOTS = 2
BR = 4
TILE = 256
F32 = jnp.float32
BF16 = jnp.bfloat16
MESH = pl.DeviceIdType.MESH


def coefficients(scales, heights):
    rate = -1.0 / (2.0 * scales * scales)
    gain = heights / jnp.sqrt(math.sqrt(math.pi) * scales)
    return jnp.concatenate([rate, gain]).astype(F32)


def gaussians(distance, coef):
    square = distance * distance
    total = coef[4] * jnp.exp(square * coef[0])
    for member in range(1, 4):
        total = total + coef[4 + member] * jnp.exp(square * coef[member])
    return total


def params(mib=48):
    return pltpu.CompilerParams(vmem_limit_bytes=mib * 1024 * 1024)


def cost(flops, nbytes):
    return pl.CostEstimate(flops=int(flops), bytes_accessed=int(nbytes), transcendentals=0)


def wide_table_kernel(width, coef, out):
    step = 512

    def piece(at, carry):
        start = pl.multiple_of(at * step, step)
        lane = lax.broadcasted_iota(jnp.int32, (TILE, step), 1) + start
        row = lax.broadcasted_iota(jnp.int32, (TILE, step), 0)
        offset = jnp.abs(lane - row)
        distance = jnp.minimum(offset, width - offset).astype(F32)
        value = gaussians(distance, coef).astype(BF16)
        out[:, pl.ds(start, step)] = value
        out[:, pl.ds(start + width, step)] = value
        return carry

    lax.fori_loop(0, width // step, piece, 0)


def tall_table_kernel(width, coef, out):
    step = 512

    def piece(at, carry):
        start = pl.multiple_of(at * step, step)
        row = lax.broadcasted_iota(jnp.int32, (step, TILE), 0) + start
        lane = lax.broadcasted_iota(jnp.int32, (step, TILE), 1)
        offset = jnp.abs(lane - row)
        distance = jnp.minimum(offset, width - offset).astype(F32)
        value = gaussians(distance, coef).astype(BF16)
        out[pl.ds(start, step), :] = value
        out[pl.ds(start + width, step), :] = value
        return carry

    lax.fori_loop(0, width // step, piece, 0)


def table(kernel, shape, width, coef):
    return pl.pallas_call(
        functools.partial(kernel, width),
        out_shape=jax.ShapeDtypeStruct(shape, BF16),
        in_specs=[pl.BlockSpec(memory_space=pltpu.SMEM)],
        out_specs=pl.BlockSpec(memory_space=pltpu.VMEM),
        compiler_params=params(),
        cost_estimate=cost(shape[0] * shape[1] * 30, shape[0] * shape[1] * 2),
    )(coef)


def zonal_forward_kernel(count, coef, fields, lines, smooth, wide, turned, made, send, recv, keep):
    variables, rows, width = fields.shape
    strip = width // count
    batch = 3 * TILE
    me = lax.axis_index("lat")
    barrier = pltpu.get_barrier_semaphore()

    def greet(other, carry):
        @pl.when(other != me)
        def _():
            pl.semaphore_signal(barrier, inc=1, device_id={"lat": other}, device_id_type=MESH)

        return carry

    lax.fori_loop(0, count, greet, 0)
    wide_table_kernel(width, coef, wide)

    def turn(variable):
        for part in range(width // TILE):
            cells = slice(part * TILE, (part + 1) * TILE)
            turned[cells, :] = fields[variable, :, cells].T

    def block(at):
        start = pl.multiple_of(width - at * TILE, TILE)
        return jnp.dot(
            wide[:, pl.ds(start, width)], turned[...], preferred_element_type=F32
        ).astype(BF16)

    def strip_copy(other):
        return pltpu.make_async_remote_copy(
            src_ref=made.at[other],
            dst_ref=lines.at[me],
            send_sem=send.at[other],
            recv_sem=recv.at[me],
            device_id={"lat": other},
            device_id_type=MESH,
        )

    own = pltpu.make_async_copy(made.at[me], lines.at[me], keep)
    turn(0)
    pl.semaphore_wait(barrier, count - 1)
    batches = width // batch
    each = batch // strip

    def one_batch(step, carry):
        which = (me // each + batches // 2 + step) % batches
        product = jnp.concatenate([block(which * 3 + part) for part in range(3)], axis=0)
        made[pl.ds(which * each, each)] = product.reshape(each, strip, rows)

        def one_strip(at, inner):
            other = which * each + at

            @pl.when(other != me)
            def _():
                strip_copy(other).start()

            @pl.when(other == me)
            def _():
                own.start()

            return inner

        return lax.fori_loop(0, each, one_strip, carry)

    lax.fori_loop(0, batches, one_batch, 0)

    for variable in range(1, variables):
        turn(variable)

        def one_block(at, carry):
            start = pl.multiple_of(at * TILE, TILE)
            smooth[variable - 1, pl.ds(start, TILE), :] = block(at)
            return carry

        lax.fori_loop(0, width // TILE, one_block, 0)

    own.wait()

    def finish(other, carry):
        @pl.when(other != me)
        def _():
            strip_copy(other).wait_send()
            pltpu.make_async_remote_copy(
                src_ref=made.at[other],
                dst_ref=lines.at[other],
                send_sem=send.at[other],
                recv_sem=recv.at[other],
                device_id={"lat": other},
                device_id_type=MESH,
            ).wait_recv()

        return carry

    lax.fori_loop(0, count, finish, 0)


def zonal_forward(fields, coef, count):
    variables, rows, width = fields.shape
    strip = width // count
    return pl.pallas_call(
        functools.partial(zonal_forward_kernel, count),
        out_shape=(
            jax.ShapeDtypeStruct((count, strip, rows), BF16),
            jax.ShapeDtypeStruct((variables - 1, width, rows), BF16),
        ),
        in_specs=[
            pl.BlockSpec(memory_space=pltpu.SMEM),
            pl.BlockSpec(memory_space=pltpu.VMEM),
        ],
        out_specs=(
            pl.BlockSpec(memory_space=pl.ANY),
            pl.BlockSpec(memory_space=pltpu.VMEM),
        ),
        scratch_shapes=[
            pltpu.VMEM((TILE, 2 * width), BF16),
            pltpu.VMEM((width, rows), BF16),
            pltpu.VMEM((count, strip, rows), BF16),
            pltpu.SemaphoreType.DMA((count,)),
            pltpu.SemaphoreType.DMA((count,)),
            pltpu.SemaphoreType.DMA,
        ],
        compiler_params=pltpu.CompilerParams(
            vmem_limit_bytes=48 * 1024 * 1024, collective_id=0, has_side_effects=True
        ),
        cost_estimate=cost(2 * variables * rows * width * width, 10 * rows * width),
    )(coef, fields)


def zonal_backward_kernel(width, lines, tall, *rest):
    out, turned = rest[-2:]
    at = pl.program_id(0)

    @pl.when(at == 0)
    def _():
        for part in range(width // TILE):
            cells = slice(part * TILE, (part + 1) * TILE)
            turned[:, cells] = lines[cells, :].T

    start = pl.multiple_of(width - at * TILE, TILE)
    out[0] = jnp.dot(turned[...], tall[pl.ds(start, width), :], preferred_element_type=F32)


def zonal_backward(lines, tall, variables, variable, gradient):
    width, rows = lines.shape
    operands = [lines, tall]
    in_specs = [
        pl.BlockSpec((width, rows), lambda at: (0, 0)),
        pl.BlockSpec((2 * width, TILE), lambda at: (0, 0)),
    ]
    aliases = {}
    if gradient is not None:
        operands.append(gradient)
        in_specs.append(pl.BlockSpec(memory_space=pl.ANY))
        aliases = {2: 0}
    return pl.pallas_call(
        functools.partial(zonal_backward_kernel, width),
        out_shape=jax.ShapeDtypeStruct((variables, rows, width), F32),
        grid=(width // TILE,),
        in_specs=in_specs,
        out_specs=pl.BlockSpec((1, rows, TILE), lambda at: (variable, 0, at)),
        scratch_shapes=[pltpu.VMEM((rows, width), BF16)],
        input_output_aliases=aliases,
        compiler_params=params(),
        cost_estimate=cost(2 * rows * width * width, 12 * rows * width),
    )(*operands)


def band_kernel(group, coef, lanes, out):
    pair, band_rows = 2, out.shape[1] // (2 * group)
    columns = out.shape[2]
    base = pl.program_id(0) * pair * band_rows
    row = lax.broadcasted_iota(jnp.int32, (pair * band_rows, columns), 0) + base
    apart = jnp.abs(row - lanes[...]).astype(F32)
    value = gaussians(apart, coef).reshape(pair, 1, band_rows, columns)
    full = jnp.broadcast_to(value, (pair, group, band_rows, columns))
    level = lax.broadcasted_iota(jnp.int32, full.shape, 1)
    lane = lax.broadcasted_iota(jnp.int32, (1, 1, 1, columns), 3) % group
    full = jnp.where(lane == level, full, 0.0)
    out[0] = full.reshape(pair * group * band_rows, columns).astype(BF16)


def band_matrices(coef, lanes, group, band_rows, bands):
    columns = lanes.shape[1]
    rows = 2 * group * band_rows
    return pl.pallas_call(
        functools.partial(band_kernel, group),
        out_shape=jax.ShapeDtypeStruct((bands // 2, rows, columns), BF16),
        grid=(bands // 2,),
        in_specs=[
            pl.BlockSpec(memory_space=pltpu.SMEM),
            pl.BlockSpec((1, columns), lambda at: (0, 0)),
        ],
        out_specs=pl.BlockSpec((1, rows, columns), lambda at: (at, 0, 0)),
        compiler_params=params(),
        cost_estimate=cost(5 * bands * rows * columns, bands * rows * columns),
    )(coef, lanes)


def meridional_forward_kernel(lines, matrix, out, total):
    at = pl.program_id(0)
    groups, strip, columns = total.shape
    part = lines.shape[2] // groups
    owners, share = out.shape[0], columns // out.shape[0]
    for group in range(groups):
        cells = slice(group * part, (group + 1) * part)
        both = jnp.concatenate([lines[0, :, cells], lines[1, :, cells]], axis=1)
        product = jnp.dot(both, matrix[0], preferred_element_type=F32)

        @pl.when(at == 0)
        def _():
            total[group] = product

        @pl.when(at > 0)
        def _():
            total[group] += product

    @pl.when(at == pl.num_programs(0) - 1)
    def _():
        for owner in range(owners):
            for group in range(groups):
                out[owner, :, group * share : (group + 1) * share] = total[
                    group, :, owner * share : (owner + 1) * share
                ].astype(BF16)


def meridional_forward(lines, matrices, owners, groups):
    bands, strip, rows = lines.shape
    pairs, depth, columns = matrices.shape
    return pl.pallas_call(
        meridional_forward_kernel,
        out_shape=jax.ShapeDtypeStruct((owners, strip, groups * columns // owners), BF16),
        grid=(pairs,),
        in_specs=[
            pl.BlockSpec((2, strip, rows), lambda at: (at, 0, 0)),
            pl.BlockSpec((1, depth, columns), lambda at: (at, 0, 0)),
        ],
        out_specs=pl.BlockSpec(
            (owners, strip, groups * columns // owners), lambda at: (0, 0, 0)
        ),
        scratch_shapes=[pltpu.VMEM((groups, strip, columns), F32)],
        compiler_params=params(),
        cost_estimate=cost(2 * bands * strip * rows * columns, 2 * bands * strip * rows),
    )(lines, matrices)


def meridional_backward_kernel(groups, own, other, matrix, out):
    share = own.shape[1] // groups
    part = out.shape[2] // groups
    for group in range(groups):
        cells = slice(group * share, (group + 1) * share)
        both = jnp.concatenate([own[:, cells], other[:, cells]], axis=1)
        product = lax.dot_general(
            both, matrix[0], (((1,), (1,)), ((), ())), preferred_element_type=F32
        ).astype(BF16)
        for band in range(2):
            out[band, :, group * part : (group + 1) * part] = product[
                :, band * part : (band + 1) * part
            ]


def meridional_backward(own, other, matrices, groups):
    pairs, depth, columns = matrices.shape
    strip, share = own.shape
    rows = depth * groups // 2
    half = pl.BlockSpec((strip, share), lambda at: (0, 0))
    return pl.pallas_call(
        functools.partial(meridional_backward_kernel, groups),
        out_shape=jax.ShapeDtypeStruct((2 * pairs, strip, rows), BF16),
        grid=(pairs,),
        in_specs=[half, half, pl.BlockSpec((1, depth, columns), lambda at: (at, 0, 0))],
        out_specs=pl.BlockSpec((2, strip, rows), lambda at: (at, 0, 0)),
        compiler_params=params(),
        cost_estimate=cost(4 * pairs * strip * rows * columns, 4 * pairs * strip * rows),
    )(own, other, matrices)


def reports_kernel(variable, group, kept_rows, own, other, ids, numbers, cells, weights, maps, departure, lifted, total):
    at = pl.program_id(0)
    strip, columns = own.shape
    block = ids.shape[0]
    levels = maps.shape[2]
    across = lax.broadcasted_iota(jnp.int32, (block, strip), 1)
    cell = ids[:, 0:1]
    down = lax.broadcasted_iota(jnp.int32, (strip, block), 0)
    place = cells[...]
    sides = []
    turned = []
    for side in range(2):
        value = jnp.where(across == cell, numbers[:, 2 * side : 2 * side + 1], 0.0)
        value = jnp.where(across == cell + 1, numbers[:, 2 * side + 1 : 2 * side + 2], value)
        sides.append(value.astype(BF16))
        value = jnp.where(down == place, weights[2 * side : 2 * side + 1, :], 0.0)
        value = jnp.where(down == place + 1, weights[2 * side + 1 : 2 * side + 2, :], value)
        turned.append(value.astype(BF16))
    level = ids[:, 2:3] - variable * levels
    chosen = jnp.where(lax.broadcasted_iota(jnp.int32, (block, levels), 1) == level, 1.0, 0.0)
    chosen = chosen.astype(BF16)
    lane = lax.broadcasted_iota(jnp.int32, (block, columns), 1) // group % kept_rows
    hits = [lane == ids[:, 1:2], lane == ids[:, 1:2] + 1]
    fields = (own, other)
    model = jnp.zeros((block, 1), F32)
    kept = []
    for half in range(2):
        mapped = jnp.dot(chosen, maps[0, half], preferred_element_type=F32)
        found = jnp.zeros((block, columns), F32)
        for side in range(2):
            picked = jnp.where(hits[side], mapped, 0.0)
            kept.append(picked)
            values = jnp.dot(sides[side], fields[half][...], preferred_element_type=F32)
            found = found + values * picked
        model = model + jnp.sum(found, axis=1, keepdims=True)
    result = numbers[:, 5:6] * (model - numbers[:, 4:5])
    both = jnp.concatenate(turned, axis=1)
    departure[...] = jnp.broadcast_to(result, (block, 128)).T[0:1, :]
    for half in range(2):
        pushes = [(kept[2 * half + side] * result).astype(BF16) for side in range(2)]
        product = jnp.dot(both, jnp.concatenate(pushes, axis=0), preferred_element_type=F32)

        @pl.when(at == 0)
        def _():
            total[half] = product

        @pl.when(at > 0)
        def _():
            total[half] += product

    @pl.when(at == pl.num_programs(0) - 1)
    def _():
        lifted[...] = total[...].astype(BF16)


def at_reports(variable, group, kept_rows, own, other, ids, numbers, cells, weights, maps):
    strip, columns = own.shape
    reports = ids.shape[0]
    block = math.gcd(reports, 256)
    half = pl.BlockSpec((strip, columns), lambda at: (0, 0))
    return pl.pallas_call(
        functools.partial(reports_kernel, variable, group, kept_rows),
        out_shape=(
            jax.ShapeDtypeStruct((1, reports), F32),
            jax.ShapeDtypeStruct((2, strip, columns), BF16),
        ),
        grid=(reports // block,),
        in_specs=[
            half,
            half,
            pl.BlockSpec((block, ids.shape[1]), lambda at: (at, 0)),
            pl.BlockSpec((block, numbers.shape[1]), lambda at: (at, 0)),
            pl.BlockSpec((1, block), lambda at: (0, at)),
            pl.BlockSpec((4, block), lambda at: (0, at)),
            pl.BlockSpec((1,) + maps.shape[1:], lambda at: (variable, 0, 0, 0)),
        ],
        out_specs=(
            pl.BlockSpec((1, block), lambda at: (0, at)),
            pl.BlockSpec((2, strip, columns), lambda at: (0, 0, 0)),
        ),
        scratch_shapes=[pltpu.VMEM((2, strip, columns), F32)],
        compiler_params=params(),
        cost_estimate=cost(16 * reports * 256 * columns, 4 * reports * 128),
    )(own, other, ids, numbers, cells, weights, maps)


def on_device(
    control,
    zonal_scales,
    zonal_heights,
    meridional_scales,
    meridional_heights,
    vertical_map,
    send_blocks,
    report_slot,
    report_level,
    report_corner,
    report_weight,
    innovation,
    report_precision,
):
    lat_count = lax.axis_size("lat")
    owners = lax.axis_size("obs")
    variables, share, band_rows, width = control.shape
    strip = width // lat_count
    all_rows = band_rows * lat_count
    levels = share * owners
    slots = owners * SLOTS
    kept = slots * BR
    points = strip * kept
    reports = report_slot.shape[-1]

    zonal = coefficients(zonal_scales, zonal_heights)
    fields = control.reshape(variables, share * band_rows, width)
    arrived, smooth = zonal_forward(fields, zonal, lat_count)

    group = 128 // band_rows
    groups = share // group
    me = lax.axis_index("obs")
    partner = [(0, 1), (1, 0)]
    blocks = lax.all_gather(send_blocks.reshape(owners, SLOTS), "obs", axis=0)
    source = jnp.arange(owners)[:, None, None]
    starts = jnp.transpose(source * (all_rows // owners) + blocks * BR, (1, 0, 2))
    starts = jnp.where(me == 0, starts, starts[::-1])
    rows = starts[..., None] + jnp.arange(BR)
    lanes = jnp.repeat(rows.reshape(-1), group).reshape(1, -1).astype(jnp.int32)
    meridional = coefficients(meridional_scales, meridional_heights)
    matrices = band_matrices(meridional, lanes, group, band_rows, lat_count)

    slot = report_slot.reshape(1, reports)
    code = report_level.reshape(1, reports)
    first = report_corner.reshape(4, reports)[0:1]
    weight = report_weight.reshape(4, reports)
    cells = first % strip
    ids = jnp.concatenate([cells, slot * BR + first // strip, code], axis=0).T
    numbers = jnp.concatenate(
        [weight, innovation.reshape(1, reports), report_precision.reshape(1, reports)], axis=0
    ).T
    maps = vertical_map.reshape(variables, levels, owners, groups, 1, group)
    maps = maps.transpose(0, 2, 1, 3, 4, 5)
    maps = jnp.where(me == 0, maps, maps[:, ::-1])
    maps = jnp.broadcast_to(maps, (variables, owners, levels, groups, kept, group))
    maps = maps.reshape(variables, owners, levels, groups * kept * group)
    tall = table(tall_table_kernel, (2 * width, TILE), width, zonal)

    sent = [arrived]
    for variable in range(1, variables):
        part = smooth[variable - 1].reshape(lat_count, strip, -1)
        sent.append(lax.all_to_all(part, "lat", split_axis=0, concat_axis=0, tiled=True))

    departures = []
    lines = []
    for variable in range(variables):
        mixed = meridional_forward(sent[variable], matrices, owners, groups)
        theirs = lax.ppermute(mixed[1], "obs", partner)
        departure, lifted = at_reports(
            variable, group, kept, mixed[0], theirs, ids, numbers, cells, weight, maps
        )
        departures.append(departure)
        theirs = lax.ppermute(lifted[1], "obs", partner)
        back = meridional_backward(lifted[0], theirs, matrices, groups)
        lines.append(lax.all_to_all(back, "lat", split_axis=0, concat_axis=0, tiled=True))

    gradient = None
    for variable in range(variables):
        gradient = zonal_backward(
            lines[variable].reshape(width, -1), tall, variables, variable, gradient
        )
    departure = departures[0]
    for variable in range(1, variables):
        departure = jnp.where(code >= variable * levels, departures[variable], departure)
    return (departure.reshape(report_slot.shape), gradient.reshape(control.shape))


def solution(mesh):
    in_specs = (
        P(None, "obs", "lat", None),
        P(),
        P(),
        P(),
        P(),
        P(),
        P("lat", "obs", None, None),
        P("lat", "obs", None),
        P("lat", "obs", None),
        P("lat", "obs", None, None),
        P("lat", "obs", None, None),
        P("lat", "obs", None),
        P("lat", "obs", None),
    )
    out_specs = (P("lat", "obs", None), P(None, "obs", "lat", None))
    return jax.shard_map(
        on_device, mesh=mesh, in_specs=in_specs, out_specs=out_specs, check_vma=False
    )
```

```python
import functools
import math

import jax
import jax.numpy as jnp
from jax import lax
from jax.experimental import pallas as pl
from jax.experimental.pallas import tpu as pltpu
from jax.sharding import PartitionSpec as P

SLOTS = 2
BR = 4
TILE = 256
F32 = jnp.float32
BF16 = jnp.bfloat16
MESH = pl.DeviceIdType.MESH


def coefficients(scales, heights):
    rate = -1.0 / (2.0 * scales * scales)
    gain = heights / jnp.sqrt(math.sqrt(math.pi) * scales)
    return jnp.concatenate([rate, gain]).astype(F32)


def gaussians(distance, coef):
    square = distance * distance
    total = coef[4] * jnp.exp(square * coef[0])
    for member in range(1, 4):
        total = total + coef[4 + member] * jnp.exp(square * coef[member])
    return total


def params(mib=48):
    return pltpu.CompilerParams(vmem_limit_bytes=mib * 1024 * 1024)


def cost(flops, nbytes):
    return pl.CostEstimate(flops=int(flops), bytes_accessed=int(nbytes), transcendentals=0)


def wide_table_kernel(width, coef, out):
    step = 512

    def piece(at, carry):
        start = pl.multiple_of(at * step, step)
        lane = lax.broadcasted_iota(jnp.int32, (TILE, step), 1) + start
        row = lax.broadcasted_iota(jnp.int32, (TILE, step), 0)
        offset = jnp.abs(lane - row)
        distance = jnp.minimum(offset, width - offset).astype(F32)
        value = gaussians(distance, coef).astype(BF16)
        out[:, pl.ds(start, step)] = value
        out[:, pl.ds(start + width, step)] = value
        return carry

    lax.fori_loop(0, width // step, piece, 0)


def tall_table_kernel(width, coef, out):
    step = 512

    def piece(at, carry):
        start = pl.multiple_of(at * step, step)
        row = lax.broadcasted_iota(jnp.int32, (step, TILE), 0) + start
        lane = lax.broadcasted_iota(jnp.int32, (step, TILE), 1)
        offset = jnp.abs(lane - row)
        distance = jnp.minimum(offset, width - offset).astype(F32)
        value = gaussians(distance, coef).astype(BF16)
        out[pl.ds(start, step), :] = value
        out[pl.ds(start + width, step), :] = value
        return carry

    lax.fori_loop(0, width // step, piece, 0)


def table(kernel, shape, width, coef):
    return pl.pallas_call(
        functools.partial(kernel, width),
        out_shape=jax.ShapeDtypeStruct(shape, BF16),
        in_specs=[pl.BlockSpec(memory_space=pltpu.SMEM)],
        out_specs=pl.BlockSpec(memory_space=pltpu.VMEM),
        compiler_params=params(),
        cost_estimate=cost(shape[0] * shape[1] * 30, shape[0] * shape[1] * 2),
    )(coef)


def zonal_forward_kernel(count, coef, fields, lines, smooth, wide, turned, made, send, recv, keep):
    variables, rows, width = fields.shape
    strip = width // count
    batch = 3 * TILE
    me = lax.axis_index("lat")
    barrier = pltpu.get_barrier_semaphore()

    def greet(other, carry):
        @pl.when(other != me)
        def _():
            pl.semaphore_signal(barrier, inc=1, device_id={"lat": other}, device_id_type=MESH)

        return carry

    lax.fori_loop(0, count, greet, 0)
    wide_table_kernel(width, coef, wide)

    def turn(variable):
        for part in range(width // TILE):
            cells = slice(part * TILE, (part + 1) * TILE)
            turned[cells, :] = fields[variable, :, cells].T

    def block(at):
        start = pl.multiple_of(width - at * TILE, TILE)
        return jnp.dot(
            wide[:, pl.ds(start, width)], turned[...], preferred_element_type=F32
        ).astype(BF16)

    def strip_copy(other):
        return pltpu.make_async_remote_copy(
            src_ref=made.at[other],
            dst_ref=lines.at[me],
            send_sem=send.at[other],
            recv_sem=recv.at[me],
            device_id={"lat": other},
            device_id_type=MESH,
        )

    own = pltpu.make_async_copy(made.at[me], lines.at[me], keep)
    turn(0)
    pl.semaphore_wait(barrier, count - 1)
    batches = width // batch
    each = batch // strip

    def one_batch(step, carry):
        which = (me // each + batches // 2 + step) % batches
        product = jnp.concatenate([block(which * 3 + part) for part in range(3)], axis=0)
        made[pl.ds(which * each, each)] = product.reshape(each, strip, rows)

        def one_strip(at, inner):
            other = which * each + at

            @pl.when(other != me)
            def _():
                strip_copy(other).start()

            @pl.when(other == me)
            def _():
                own.start()

            return inner

        return lax.fori_loop(0, each, one_strip, carry)

    lax.fori_loop(0, batches, one_batch, 0)

    for variable in range(1, variables):
        turn(variable)

        def one_block(at, carry):
            start = pl.multiple_of(at * TILE, TILE)
            smooth[variable - 1, pl.ds(start, TILE), :] = block(at)
            return carry

        lax.fori_loop(0, width // TILE, one_block, 0)

    own.wait()

    def finish(other, carry):
        @pl.when(other != me)
        def _():
            strip_copy(other).wait_send()
            pltpu.make_async_remote_copy(
                src_ref=made.at[other],
                dst_ref=lines.at[other],
                send_sem=send.at[other],
                recv_sem=recv.at[other],
                device_id={"lat": other},
                device_id_type=MESH,
            ).wait_recv()

        return carry

    lax.fori_loop(0, count, finish, 0)


def zonal_forward(fields, coef, count):
    variables, rows, width = fields.shape
    strip = width // count
    return pl.pallas_call(
        functools.partial(zonal_forward_kernel, count),
        out_shape=(
            jax.ShapeDtypeStruct((count, strip, rows), BF16),
            jax.ShapeDtypeStruct((variables - 1, width, rows), BF16),
        ),
        in_specs=[
            pl.BlockSpec(memory_space=pltpu.SMEM),
            pl.BlockSpec(memory_space=pltpu.VMEM),
        ],
        out_specs=(
            pl.BlockSpec(memory_space=pl.ANY),
            pl.BlockSpec(memory_space=pltpu.VMEM),
        ),
        scratch_shapes=[
            pltpu.VMEM((TILE, 2 * width), BF16),
            pltpu.VMEM((width, rows), BF16),
            pltpu.VMEM((count, strip, rows), BF16),
            pltpu.SemaphoreType.DMA((count,)),
            pltpu.SemaphoreType.DMA((count,)),
            pltpu.SemaphoreType.DMA,
        ],
        compiler_params=pltpu.CompilerParams(
            vmem_limit_bytes=48 * 1024 * 1024, collective_id=0, has_side_effects=True
        ),
        cost_estimate=cost(2 * variables * rows * width * width, 10 * rows * width),
    )(coef, fields)


def zonal_backward_kernel(width, lines, tall, *rest):
    out, turned = rest[-2:]
    at = pl.program_id(0)

    @pl.when(at == 0)
    def _():
        for part in range(width // TILE):
            cells = slice(part * TILE, (part + 1) * TILE)
            turned[:, cells] = lines[cells, :].T

    start = pl.multiple_of(width - at * TILE, TILE)
    out[0] = jnp.dot(turned[...], tall[pl.ds(start, width), :], preferred_element_type=F32)


def zonal_backward(lines, tall, variables, variable, gradient):
    width, rows = lines.shape
    operands = [lines, tall]
    in_specs = [
        pl.BlockSpec((width, rows), lambda at: (0, 0)),
        pl.BlockSpec((2 * width, TILE), lambda at: (0, 0)),
    ]
    aliases = {}
    if gradient is not None:
        operands.append(gradient)
        in_specs.append(pl.BlockSpec(memory_space=pl.ANY))
        aliases = {2: 0}
    return pl.pallas_call(
        functools.partial(zonal_backward_kernel, width),
        out_shape=jax.ShapeDtypeStruct((variables, rows, width), F32),
        grid=(width // TILE,),
        in_specs=in_specs,
        out_specs=pl.BlockSpec((1, rows, TILE), lambda at: (variable, 0, at)),
        scratch_shapes=[pltpu.VMEM((rows, width), BF16)],
        input_output_aliases=aliases,
        compiler_params=params(),
        cost_estimate=cost(2 * rows * width * width, 12 * rows * width),
    )(*operands)


def band_kernel(group, coef, lanes, out):
    pair, band_rows = 2, out.shape[1] // (2 * group)
    columns = out.shape[2]
    base = pl.program_id(0) * pair * band_rows
    row = lax.broadcasted_iota(jnp.int32, (pair * band_rows, columns), 0) + base
    apart = jnp.abs(row - lanes[...]).astype(F32)
    value = gaussians(apart, coef).reshape(pair, 1, band_rows, columns)
    full = jnp.broadcast_to(value, (pair, group, band_rows, columns))
    level = lax.broadcasted_iota(jnp.int32, full.shape, 1)
    lane = lax.broadcasted_iota(jnp.int32, (1, 1, 1, columns), 3) % group
    full = jnp.where(lane == level, full, 0.0)
    out[0] = full.reshape(pair * group * band_rows, columns).astype(BF16)


def band_matrices(coef, lanes, group, band_rows, bands):
    columns = lanes.shape[1]
    rows = 2 * group * band_rows
    return pl.pallas_call(
        functools.partial(band_kernel, group),
        out_shape=jax.ShapeDtypeStruct((bands // 2, rows, columns), BF16),
        grid=(bands // 2,),
        in_specs=[
            pl.BlockSpec(memory_space=pltpu.SMEM),
            pl.BlockSpec((1, columns), lambda at: (0, 0)),
        ],
        out_specs=pl.BlockSpec((1, rows, columns), lambda at: (at, 0, 0)),
        compiler_params=params(),
        cost_estimate=cost(5 * bands * rows * columns, bands * rows * columns),
    )(coef, lanes)


def middle_kernel(
    variable,
    group,
    kept_rows,
    parcels,
    lines,
    matrices,
    ids,
    numbers,
    cells,
    weights,
    maps,
    landed,
    back,
    departure,
    mixing,
    mixed,
    mixed_other,
    total,
    lifted,
    lifted_other,
    send,
    recv,
    keep,
    pair_send,
    pair_recv,
):
    count, strip, depth = lines.shape
    groups = mixing.shape[0]
    part = depth // groups
    columns = mixed.shape[2]
    share = columns // groups
    levels = maps.shape[1]
    reports = ids.shape[0]
    block = math.gcd(reports, 256)
    me = lax.axis_index("lat")
    twin = 1 - lax.axis_index("obs")
    barrier = pltpu.get_barrier_semaphore()
    pl.semaphore_signal(barrier, inc=1, device_id={"obs": twin}, device_id_type=MESH)

    def greet(other, carry):
        @pl.when(other != me)
        def _():
            pl.semaphore_signal(barrier, inc=1, device_id={"lat": other}, device_id_type=MESH)

        return carry

    lax.fori_loop(0, count, greet, 0)
    own = pltpu.make_async_copy(parcels.at[me], landed.at[me], keep)
    own.start()
    mixing[...] = jnp.zeros_like(mixing)
    total[...] = jnp.zeros_like(total)
    pl.semaphore_wait(barrier, count)

    def parcel(other, slot):
        return pltpu.make_async_remote_copy(
            src_ref=parcels.at[other],
            dst_ref=landed.at[slot],
            send_sem=send.at[other],
            recv_sem=recv.at[slot],
            device_id={"lat": other},
            device_id_type=MESH,
        )

    def begin(step, carry):
        other = (me + count // 2 + step) % count

        @pl.when(other != me)
        def _():
            parcel(other, me).start()

        return carry

    lax.fori_loop(0, count, begin, 0)

    def mix(pair, carry):
        for at in range(groups):
            lane = slice(at * part, (at + 1) * part)
            both = jnp.concatenate([lines[2 * pair, :, lane], lines[2 * pair + 1, :, lane]], axis=1)
            mixing[at] += jnp.dot(both, matrices[pair], preferred_element_type=F32)
        return carry

    lax.fori_loop(0, count // 2, mix, 0)
    for owner in (1, 0):
        for at in range(groups):
            mixed[owner, :, at * share : (at + 1) * share] = mixing[
                at, :, owner * share : (owner + 1) * share
            ].astype(BF16)
    trade = pltpu.make_async_remote_copy(
        src_ref=mixed.at[1],
        dst_ref=mixed_other,
        send_sem=pair_send.at[0],
        recv_sem=pair_recv.at[0],
        device_id={"obs": twin},
        device_id_type=MESH,
    )
    trade.start()
    trade.wait()

    def observe(at, carry):
        start = pl.multiple_of(at * block, block)
        here = pl.ds(start, block)
        across = lax.broadcasted_iota(jnp.int32, (block, strip), 1)
        down = lax.broadcasted_iota(jnp.int32, (strip, block), 0)
        cell = ids[here, 0:1]
        row = ids[here, 1:2]
        place = cells[0:1, here]
        sides = []
        turned = []
        for side in range(2):
            low, high = 2 * side, 2 * side + 1
            value = jnp.where(across == cell, numbers[here, low : low + 1], 0.0)
            value = jnp.where(across == cell + 1, numbers[here, high : high + 1], value)
            sides.append(value.astype(BF16))
            value = jnp.where(down == place, weights[low : low + 1, here], 0.0)
            value = jnp.where(down == place + 1, weights[high : high + 1, here], value)
            turned.append(value.astype(BF16))
        both = jnp.concatenate(turned, axis=1)
        level = ids[here, 2:3] - variable * levels
        chosen = jnp.where(lax.broadcasted_iota(jnp.int32, (block, levels), 1) == level, 1.0, 0.0)
        chosen = chosen.astype(BF16)
        lane = lax.broadcasted_iota(jnp.int32, (block, columns), 1) // group % kept_rows
        hits = [lane == row, lane == row + 1]
        model = jnp.zeros((block, 1), F32)
        kept = []
        for half in range(2):
            field = mixed[0] if half == 0 else mixed_other[...]
            mapped = jnp.dot(chosen, maps[half], preferred_element_type=F32)
            found = jnp.zeros((block, columns), F32)
            for side in range(2):
                picked = jnp.where(hits[side], mapped, 0.0)
                kept.append(picked)
                values = jnp.dot(sides[side], field, preferred_element_type=F32)
                found = found + values * picked
            model = model + jnp.sum(found, axis=1, keepdims=True)
        result = numbers[here, 5:6] * (model - numbers[here, 4:5])
        departure[0:1, here] = jnp.broadcast_to(result, (block, 128)).T[0:1, :]
        for half in range(2):
            pushes = [(kept[2 * half + side] * result).astype(BF16) for side in range(2)]
            total[half] += jnp.dot(
                both, jnp.concatenate(pushes, axis=0), preferred_element_type=F32
            )
        return carry

    lax.fori_loop(0, reports // block, observe, 0)
    lifted[...] = total[...].astype(BF16)
    trade = pltpu.make_async_remote_copy(
        src_ref=lifted.at[1],
        dst_ref=lifted_other,
        send_sem=pair_send.at[1],
        recv_sem=pair_recv.at[1],
        device_id={"obs": twin},
        device_id_type=MESH,
    )
    trade.start()
    trade.wait()

    def unmix(pair, carry):
        for at in range(groups):
            lane = slice(at * share, (at + 1) * share)
            both = jnp.concatenate([lifted[0, :, lane], lifted_other[:, lane]], axis=1)
            product = lax.dot_general(
                both, matrices[pair], (((1,), (1,)), ((), ())), preferred_element_type=F32
            ).astype(BF16)
            for band in range(2):
                back[2 * pair + band, :, at * part : (at + 1) * part] = product[
                    :, band * part : (band + 1) * part
                ]
        return carry

    lax.fori_loop(0, count // 2, unmix, 0)
    own.wait()

    def finish(other, carry):
        @pl.when(other != me)
        def _():
            parcel(other, me).wait_send()
            parcel(other, other).wait_recv()

        return carry

    lax.fori_loop(0, count, finish, 0)


def middle(variable, group, kept_rows, parcels, lines, matrices, ids, numbers, cells, weights, maps):
    count, strip, depth = lines.shape
    columns = matrices.shape[2]
    groups = maps.shape[2] // columns * 2
    reports = ids.shape[0]
    width = maps.shape[2]
    vmem = pl.BlockSpec(memory_space=pltpu.VMEM)
    return pl.pallas_call(
        functools.partial(middle_kernel, variable, group, kept_rows),
        out_shape=(
            jax.ShapeDtypeStruct(lines.shape, BF16),
            jax.ShapeDtypeStruct(lines.shape, BF16),
            jax.ShapeDtypeStruct((1, reports), F32),
        ),
        in_specs=[pl.BlockSpec(memory_space=pl.ANY)] + [vmem] * 7,
        out_specs=(pl.BlockSpec(memory_space=pl.ANY), vmem, vmem),
        scratch_shapes=[
            pltpu.VMEM((groups, strip, columns), F32),
            pltpu.VMEM((2, strip, width), BF16),
            pltpu.VMEM((strip, width), BF16),
            pltpu.VMEM((2, strip, width), F32),
            pltpu.VMEM((2, strip, width), BF16),
            pltpu.VMEM((strip, width), BF16),
            pltpu.SemaphoreType.DMA((count,)),
            pltpu.SemaphoreType.DMA((count,)),
            pltpu.SemaphoreType.DMA,
            pltpu.SemaphoreType.DMA((2,)),
            pltpu.SemaphoreType.DMA((2,)),
        ],
        compiler_params=pltpu.CompilerParams(
            vmem_limit_bytes=48 * 1024 * 1024,
            collective_id=1 + variable,
            has_side_effects=True,
        ),
        cost_estimate=cost(20 * reports * 256 * width, 8 * count * strip * depth),
    )(parcels, lines, matrices, ids, numbers, cells, weights, maps)


def on_device(
    control,
    zonal_scales,
    zonal_heights,
    meridional_scales,
    meridional_heights,
    vertical_map,
    send_blocks,
    report_slot,
    report_level,
    report_corner,
    report_weight,
    innovation,
    report_precision,
):
    lat_count = lax.axis_size("lat")
    owners = lax.axis_size("obs")
    variables, share, band_rows, width = control.shape
    strip = width // lat_count
    all_rows = band_rows * lat_count
    levels = share * owners
    slots = owners * SLOTS
    kept = slots * BR
    points = strip * kept
    reports = report_slot.shape[-1]

    zonal = coefficients(zonal_scales, zonal_heights)
    fields = control.reshape(variables, share * band_rows, width)
    arrived, smooth = zonal_forward(fields, zonal, lat_count)

    group = 128 // band_rows
    groups = share // group
    me = lax.axis_index("obs")
    blocks = lax.all_gather(send_blocks.reshape(owners, SLOTS), "obs", axis=0)
    source = jnp.arange(owners)[:, None, None]
    starts = jnp.transpose(source * (all_rows // owners) + blocks * BR, (1, 0, 2))
    starts = jnp.where(me == 0, starts, starts[::-1])
    rows = starts[..., None] + jnp.arange(BR)
    lanes = jnp.repeat(rows.reshape(-1), group).reshape(1, -1).astype(jnp.int32)
    meridional = coefficients(meridional_scales, meridional_heights)
    matrices = band_matrices(meridional, lanes, group, band_rows, lat_count)

    slot = report_slot.reshape(1, reports)
    code = report_level.reshape(1, reports)
    first = report_corner.reshape(4, reports)[0:1]
    weight = report_weight.reshape(4, reports)
    cells = first % strip
    ids = jnp.concatenate([cells, slot * BR + first // strip, code], axis=0).T
    numbers = jnp.concatenate(
        [weight, innovation.reshape(1, reports), report_precision.reshape(1, reports)], axis=0
    ).T
    maps = vertical_map.reshape(variables, levels, owners, groups, 1, group)
    maps = maps.transpose(0, 2, 1, 3, 4, 5)
    maps = jnp.where(me == 0, maps, maps[:, ::-1])
    maps = jnp.broadcast_to(maps, (variables, owners, levels, groups, kept, group))
    maps = maps.reshape(variables, owners, levels, groups * kept * group)
    tall = table(tall_table_kernel, (2 * width, TILE), width, zonal)

    parcels = [
        smooth[variable].reshape(lat_count, strip, -1) for variable in range(variables - 1)
    ]
    landed = [arrived]
    departures = []
    for variable in range(variables):
        there, back, departure = middle(
            variable,
            group,
            kept,
            parcels[variable],
            landed[variable],
            matrices,
            ids,
            numbers,
            cells,
            weight,
            maps[variable],
        )
        parcels.append(back)
        landed.append(there)
        departures.append(departure)
    lines = landed[variables:]
    for part in parcels[variables:]:
        lines.append(lax.all_to_all(part, "lat", split_axis=0, concat_axis=0, tiled=True))

    gradient = None
    for variable in range(variables):
        gradient = zonal_backward(
            lines[variable].reshape(width, -1), tall, variables, variable, gradient
        )
    departure = departures[0]
    for variable in range(1, variables):
        departure = jnp.where(code >= variable * levels, departures[variable], departure)
    return (departure.reshape(report_slot.shape), gradient.reshape(control.shape))


def solution(mesh):
    in_specs = (
        P(None, "obs", "lat", None),
        P(),
        P(),
        P(),
        P(),
        P(),
        P("lat", "obs", None, None),
        P("lat", "obs", None),
        P("lat", "obs", None),
        P("lat", "obs", None, None),
        P("lat", "obs", None, None),
        P("lat", "obs", None),
        P("lat", "obs", None),
    )
    out_specs = (P("lat", "obs", None), P(None, "obs", "lat", None))
    return jax.shard_map(
        on_device, mesh=mesh, in_specs=in_specs, out_specs=out_specs, check_vma=False
    )
```

```python
import functools
import math

import jax
import jax.numpy as jnp
from jax import lax
from jax.experimental import pallas as pl
from jax.experimental.pallas import tpu as pltpu
from jax.sharding import PartitionSpec as P

SLOTS = 2
BR = 4
TILE = 256
F32 = jnp.float32
BF16 = jnp.bfloat16
MESH = pl.DeviceIdType.MESH


def coefficients(scales, heights):
    rate = -1.0 / (2.0 * scales * scales)
    gain = heights / jnp.sqrt(math.sqrt(math.pi) * scales)
    return jnp.concatenate([rate, gain]).astype(F32)


def gaussians(distance, coef):
    square = distance * distance
    total = coef[4] * jnp.exp(square * coef[0])
    for member in range(1, 4):
        total = total + coef[4 + member] * jnp.exp(square * coef[member])
    return total


def params(mib=48):
    return pltpu.CompilerParams(vmem_limit_bytes=mib * 1024 * 1024)


def cost(flops, nbytes):
    return pl.CostEstimate(flops=int(flops), bytes_accessed=int(nbytes), transcendentals=0)


def wide_table_kernel(width, coef, out):
    step = 512

    def piece(at, carry):
        start = pl.multiple_of(at * step, step)
        lane = lax.broadcasted_iota(jnp.int32, (TILE, step), 1) + start
        row = lax.broadcasted_iota(jnp.int32, (TILE, step), 0)
        offset = jnp.abs(lane - row)
        distance = jnp.minimum(offset, width - offset).astype(F32)
        value = gaussians(distance, coef).astype(BF16)
        out[:, pl.ds(start, step)] = value
        out[:, pl.ds(start + width, step)] = value
        return carry

    lax.fori_loop(0, width // step, piece, 0)


def tall_table_kernel(width, coef, out):
    step = 512

    def piece(at, carry):
        start = pl.multiple_of(at * step, step)
        row = lax.broadcasted_iota(jnp.int32, (step, TILE), 0) + start
        lane = lax.broadcasted_iota(jnp.int32, (step, TILE), 1)
        offset = jnp.abs(lane - row)
        distance = jnp.minimum(offset, width - offset).astype(F32)
        value = gaussians(distance, coef).astype(BF16)
        out[pl.ds(start, step), :] = value
        out[pl.ds(start + width, step), :] = value
        return carry

    lax.fori_loop(0, width // step, piece, 0)


def table(kernel, shape, width, coef):
    return pl.pallas_call(
        functools.partial(kernel, width),
        out_shape=jax.ShapeDtypeStruct(shape, BF16),
        in_specs=[pl.BlockSpec(memory_space=pltpu.SMEM)],
        out_specs=pl.BlockSpec(memory_space=pltpu.VMEM),
        compiler_params=params(),
        cost_estimate=cost(shape[0] * shape[1] * 30, shape[0] * shape[1] * 2),
    )(coef)


def zonal_forward_kernel(count, coef, fields, lines, smooth, wide, turned, made, send, recv, keep):
    variables, rows, width = fields.shape
    strip = width // count
    batch = 3 * TILE
    me = lax.axis_index("lat")
    barrier = pltpu.get_barrier_semaphore()

    def greet(other, carry):
        @pl.when(other != me)
        def _():
            pl.semaphore_signal(barrier, inc=1, device_id={"lat": other}, device_id_type=MESH)

        return carry

    lax.fori_loop(0, count, greet, 0)
    wide_table_kernel(width, coef, wide)

    def turn(variable):
        for part in range(width // TILE):
            cells = slice(part * TILE, (part + 1) * TILE)
            turned[cells, :] = fields[variable, :, cells].T

    def block(at):
        start = pl.multiple_of(width - at * TILE, TILE)
        return jnp.dot(
            wide[:, pl.ds(start, width)], turned[...], preferred_element_type=F32
        ).astype(BF16)

    def strip_copy(other):
        return pltpu.make_async_remote_copy(
            src_ref=made.at[other],
            dst_ref=lines.at[me],
            send_sem=send.at[other],
            recv_sem=recv.at[me],
            device_id={"lat": other},
            device_id_type=MESH,
        )

    own = pltpu.make_async_copy(made.at[me], lines.at[me], keep)
    turn(0)
    pl.semaphore_wait(barrier, count - 1)
    batches = width // batch
    each = batch // strip

    def one_batch(step, carry):
        which = (me // each + batches // 2 + step) % batches
        product = jnp.concatenate([block(which * 3 + part) for part in range(3)], axis=0)
        made[pl.ds(which * each, each)] = product.reshape(each, strip, rows)

        def one_strip(at, inner):
            other = which * each + at

            @pl.when(other != me)
            def _():
                strip_copy(other).start()

            @pl.when(other == me)
            def _():
                own.start()

            return inner

        return lax.fori_loop(0, each, one_strip, carry)

    lax.fori_loop(0, batches, one_batch, 0)

    for variable in range(1, variables):
        turn(variable)

        def one_block(at, carry):
            start = pl.multiple_of(at * TILE, TILE)
            smooth[variable - 1, pl.ds(start, TILE), :] = block(at)
            return carry

        lax.fori_loop(0, width // TILE, one_block, 0)

    own.wait()

    def finish(other, carry):
        @pl.when(other != me)
        def _():
            strip_copy(other).wait_send()
            pltpu.make_async_remote_copy(
                src_ref=made.at[other],
                dst_ref=lines.at[other],
                send_sem=send.at[other],
                recv_sem=recv.at[other],
                device_id={"lat": other},
                device_id_type=MESH,
            ).wait_recv()

        return carry

    lax.fori_loop(0, count, finish, 0)


def zonal_forward(fields, coef, count):
    variables, rows, width = fields.shape
    strip = width // count
    return pl.pallas_call(
        functools.partial(zonal_forward_kernel, count),
        out_shape=(
            jax.ShapeDtypeStruct((count, strip, rows), BF16),
            jax.ShapeDtypeStruct((variables - 1, width, rows), BF16),
        ),
        in_specs=[
            pl.BlockSpec(memory_space=pltpu.SMEM),
            pl.BlockSpec(memory_space=pltpu.VMEM),
        ],
        out_specs=(
            pl.BlockSpec(memory_space=pl.ANY),
            pl.BlockSpec(memory_space=pltpu.VMEM),
        ),
        scratch_shapes=[
            pltpu.VMEM((TILE, 2 * width), BF16),
            pltpu.VMEM((width, rows), BF16),
            pltpu.VMEM((count, strip, rows), BF16),
            pltpu.SemaphoreType.DMA((count,)),
            pltpu.SemaphoreType.DMA((count,)),
            pltpu.SemaphoreType.DMA,
        ],
        compiler_params=pltpu.CompilerParams(
            vmem_limit_bytes=48 * 1024 * 1024, collective_id=0, has_side_effects=True
        ),
        cost_estimate=cost(2 * variables * rows * width * width, 10 * rows * width),
    )(coef, fields)


def zonal_backward_kernel(width, lines, tall, *rest):
    out, turned = rest[-2:]
    at = pl.program_id(0)

    @pl.when(at == 0)
    def _():
        for part in range(width // TILE):
            cells = slice(part * TILE, (part + 1) * TILE)
            turned[:, cells] = lines[cells, :].T

    blocks = out.shape[2] // TILE
    for part in range(blocks):
        start = pl.multiple_of(width - (at * blocks + part) * TILE, TILE)
        out[0, :, part * TILE : (part + 1) * TILE] = jnp.dot(
            turned[...], tall[pl.ds(start, width), :], preferred_element_type=F32
        )


def zonal_backward(lines, tall, variables, variable, gradient):
    width, rows = lines.shape
    batch = 3 * TILE
    operands = [lines, tall]
    in_specs = [
        pl.BlockSpec((width, rows), lambda at: (0, 0)),
        pl.BlockSpec((2 * width, TILE), lambda at: (0, 0)),
    ]
    aliases = {}
    if gradient is not None:
        operands.append(gradient)
        in_specs.append(pl.BlockSpec(memory_space=pl.ANY))
        aliases = {2: 0}
    return pl.pallas_call(
        functools.partial(zonal_backward_kernel, width),
        out_shape=jax.ShapeDtypeStruct((variables, rows, width), F32),
        grid=(width // batch,),
        in_specs=in_specs,
        out_specs=pl.BlockSpec((1, rows, batch), lambda at: (variable, 0, at)),
        scratch_shapes=[pltpu.VMEM((rows, width), BF16)],
        input_output_aliases=aliases,
        compiler_params=params(),
        cost_estimate=cost(2 * rows * width * width, 12 * rows * width),
    )(*operands)


def band_kernel(group, coef, lanes, out):
    pair, band_rows = 2, out.shape[1] // (2 * group)
    columns = out.shape[2]
    base = pl.program_id(0) * pair * band_rows
    row = lax.broadcasted_iota(jnp.int32, (pair * band_rows, columns), 0) + base
    apart = jnp.abs(row - lanes[...]).astype(F32)
    value = gaussians(apart, coef).reshape(pair, 1, band_rows, columns)
    full = jnp.broadcast_to(value, (pair, group, band_rows, columns))
    level = lax.broadcasted_iota(jnp.int32, full.shape, 1)
    lane = lax.broadcasted_iota(jnp.int32, (1, 1, 1, columns), 3) % group
    full = jnp.where(lane == level, full, 0.0)
    out[0] = full.reshape(pair * group * band_rows, columns).astype(BF16)


def band_matrices(coef, lanes, group, band_rows, bands):
    columns = lanes.shape[1]
    rows = 2 * group * band_rows
    return pl.pallas_call(
        functools.partial(band_kernel, group),
        out_shape=jax.ShapeDtypeStruct((bands // 2, rows, columns), BF16),
        grid=(bands // 2,),
        in_specs=[
            pl.BlockSpec(memory_space=pltpu.SMEM),
            pl.BlockSpec((1, columns), lambda at: (0, 0)),
        ],
        out_specs=pl.BlockSpec((1, rows, columns), lambda at: (at, 0, 0)),
        compiler_params=params(),
        cost_estimate=cost(5 * bands * rows * columns, bands * rows * columns),
    )(coef, lanes)


def meridional_forward_kernel(lines, matrix, out, total):
    at = pl.program_id(0)
    groups, strip, columns = total.shape
    part = lines.shape[2] // groups
    owners, share = out.shape[0], columns // out.shape[0]
    for group in range(groups):
        cells = slice(group * part, (group + 1) * part)
        both = jnp.concatenate([lines[0, :, cells], lines[1, :, cells]], axis=1)
        product = jnp.dot(both, matrix[0], preferred_element_type=F32)

        @pl.when(at == 0)
        def _():
            total[group] = product

        @pl.when(at > 0)
        def _():
            total[group] += product

    @pl.when(at == pl.num_programs(0) - 1)
    def _():
        for owner in range(owners):
            for group in range(groups):
                out[owner, :, group * share : (group + 1) * share] = total[
                    group, :, owner * share : (owner + 1) * share
                ].astype(BF16)


def meridional_forward(lines, matrices, owners, groups):
    bands, strip, rows = lines.shape
    pairs, depth, columns = matrices.shape
    return pl.pallas_call(
        meridional_forward_kernel,
        out_shape=jax.ShapeDtypeStruct((owners, strip, groups * columns // owners), BF16),
        grid=(pairs,),
        in_specs=[
            pl.BlockSpec((2, strip, rows), lambda at: (at, 0, 0)),
            pl.BlockSpec((1, depth, columns), lambda at: (at, 0, 0)),
        ],
        out_specs=pl.BlockSpec(
            (owners, strip, groups * columns // owners), lambda at: (0, 0, 0)
        ),
        scratch_shapes=[pltpu.VMEM((groups, strip, columns), F32)],
        compiler_params=params(),
        cost_estimate=cost(2 * bands * strip * rows * columns, 2 * bands * strip * rows),
    )(lines, matrices)


def meridional_backward_kernel(groups, own, other, matrix, out):
    share = own.shape[1] // groups
    part = out.shape[2] // groups
    for group in range(groups):
        cells = slice(group * share, (group + 1) * share)
        both = jnp.concatenate([own[:, cells], other[:, cells]], axis=1)
        product = lax.dot_general(
            both, matrix[0], (((1,), (1,)), ((), ())), preferred_element_type=F32
        ).astype(BF16)
        for band in range(2):
            out[band, :, group * part : (group + 1) * part] = product[
                :, band * part : (band + 1) * part
            ]


def meridional_backward(own, other, matrices, groups):
    pairs, depth, columns = matrices.shape
    strip, share = own.shape
    rows = depth * groups // 2
    half = pl.BlockSpec((strip, share), lambda at: (0, 0))
    return pl.pallas_call(
        functools.partial(meridional_backward_kernel, groups),
        out_shape=jax.ShapeDtypeStruct((2 * pairs, strip, rows), BF16),
        grid=(pairs,),
        in_specs=[half, half, pl.BlockSpec((1, depth, columns), lambda at: (at, 0, 0))],
        out_specs=pl.BlockSpec((2, strip, rows), lambda at: (at, 0, 0)),
        compiler_params=params(),
        cost_estimate=cost(4 * pairs * strip * rows * columns, 4 * pairs * strip * rows),
    )(own, other, matrices)


def reports_kernel(variable, group, kept_rows, own, other, ids, numbers, cells, weights, maps, departure, lifted, total):
    at = pl.program_id(0)
    strip, columns = own.shape
    block = ids.shape[0]
    levels = maps.shape[2]
    across = lax.broadcasted_iota(jnp.int32, (block, strip), 1)
    cell = ids[:, 0:1]
    down = lax.broadcasted_iota(jnp.int32, (strip, block), 0)
    place = cells[...]
    sides = []
    turned = []
    for side in range(2):
        value = jnp.where(across == cell, numbers[:, 2 * side : 2 * side + 1], 0.0)
        value = jnp.where(across == cell + 1, numbers[:, 2 * side + 1 : 2 * side + 2], value)
        sides.append(value.astype(BF16))
        value = jnp.where(down == place, weights[2 * side : 2 * side + 1, :], 0.0)
        value = jnp.where(down == place + 1, weights[2 * side + 1 : 2 * side + 2, :], value)
        turned.append(value.astype(BF16))
    level = ids[:, 2:3] - variable * levels
    chosen = jnp.where(lax.broadcasted_iota(jnp.int32, (block, levels), 1) == level, 1.0, 0.0)
    chosen = chosen.astype(BF16)
    lane = lax.broadcasted_iota(jnp.int32, (block, columns), 1) // group % kept_rows
    hits = [lane == ids[:, 1:2], lane == ids[:, 1:2] + 1]
    fields = (own, other)
    model = jnp.zeros((block, 1), F32)
    kept = []
    for half in range(2):
        mapped = jnp.dot(chosen, maps[0, half], preferred_element_type=F32)
        found = jnp.zeros((block, columns), F32)
        for side in range(2):
            picked = jnp.where(hits[side], mapped, 0.0)
            kept.append(picked)
            values = jnp.dot(sides[side], fields[half][...], preferred_element_type=F32)
            found = found + values * picked
        model = model + jnp.sum(found, axis=1, keepdims=True)
    result = numbers[:, 5:6] * (model - numbers[:, 4:5])
    both = jnp.concatenate(turned, axis=1)
    departure[...] = jnp.broadcast_to(result, (block, 128)).T[0:1, :]
    for half in range(2):
        pushes = [(kept[2 * half + side] * result).astype(BF16) for side in range(2)]
        product = jnp.dot(both, jnp.concatenate(pushes, axis=0), preferred_element_type=F32)

        @pl.when(at == 0)
        def _():
            total[half] = product

        @pl.when(at > 0)
        def _():
            total[half] += product

    @pl.when(at == pl.num_programs(0) - 1)
    def _():
        lifted[...] = total[...].astype(BF16)


def at_reports(variable, group, kept_rows, own, other, ids, numbers, cells, weights, maps):
    strip, columns = own.shape
    reports = ids.shape[0]
    block = math.gcd(reports, 256)
    half = pl.BlockSpec((strip, columns), lambda at: (0, 0))
    return pl.pallas_call(
        functools.partial(reports_kernel, variable, group, kept_rows),
        out_shape=(
            jax.ShapeDtypeStruct((1, reports), F32),
            jax.ShapeDtypeStruct((2, strip, columns), BF16),
        ),
        grid=(reports // block,),
        in_specs=[
            half,
            half,
            pl.BlockSpec((block, ids.shape[1]), lambda at: (at, 0)),
            pl.BlockSpec((block, numbers.shape[1]), lambda at: (at, 0)),
            pl.BlockSpec((1, block), lambda at: (0, at)),
            pl.BlockSpec((4, block), lambda at: (0, at)),
            pl.BlockSpec((1,) + maps.shape[1:], lambda at: (variable, 0, 0, 0)),
        ],
        out_specs=(
            pl.BlockSpec((1, block), lambda at: (0, at)),
            pl.BlockSpec((2, strip, columns), lambda at: (0, 0, 0)),
        ),
        scratch_shapes=[pltpu.VMEM((2, strip, columns), F32)],
        compiler_params=params(),
        cost_estimate=cost(16 * reports * 256 * columns, 4 * reports * 128),
    )(own, other, ids, numbers, cells, weights, maps)


def on_device(
    control,
    zonal_scales,
    zonal_heights,
    meridional_scales,
    meridional_heights,
    vertical_map,
    send_blocks,
    report_slot,
    report_level,
    report_corner,
    report_weight,
    innovation,
    report_precision,
):
    lat_count = lax.axis_size("lat")
    owners = lax.axis_size("obs")
    variables, share, band_rows, width = control.shape
    strip = width // lat_count
    all_rows = band_rows * lat_count
    levels = share * owners
    slots = owners * SLOTS
    kept = slots * BR
    points = strip * kept
    reports = report_slot.shape[-1]

    zonal = coefficients(zonal_scales, zonal_heights)
    fields = control.reshape(variables, share * band_rows, width)
    arrived, smooth = zonal_forward(fields, zonal, lat_count)

    group = 128 // band_rows
    groups = share // group
    me = lax.axis_index("obs")
    partner = [(0, 1), (1, 0)]
    blocks = lax.all_gather(send_blocks.reshape(owners, SLOTS), "obs", axis=0)
    source = jnp.arange(owners)[:, None, None]
    starts = jnp.transpose(source * (all_rows // owners) + blocks * BR, (1, 0, 2))
    starts = jnp.where(me == 0, starts, starts[::-1])
    rows = starts[..., None] + jnp.arange(BR)
    lanes = jnp.repeat(rows.reshape(-1), group).reshape(1, -1).astype(jnp.int32)
    meridional = coefficients(meridional_scales, meridional_heights)
    matrices = band_matrices(meridional, lanes, group, band_rows, lat_count)

    slot = report_slot.reshape(1, reports)
    code = report_level.reshape(1, reports)
    first = report_corner.reshape(4, reports)[0:1]
    weight = report_weight.reshape(4, reports)
    cells = first % strip
    ids = jnp.concatenate([cells, slot * BR + first // strip, code], axis=0).T
    numbers = jnp.concatenate(
        [weight, innovation.reshape(1, reports), report_precision.reshape(1, reports)], axis=0
    ).T
    maps = vertical_map.reshape(variables, levels, owners, groups, 1, group)
    maps = maps.transpose(0, 2, 1, 3, 4, 5)
    maps = jnp.where(me == 0, maps, maps[:, ::-1])
    maps = jnp.broadcast_to(maps, (variables, owners, levels, groups, kept, group))
    maps = maps.reshape(variables, owners, levels, groups * kept * group)
    tall = table(tall_table_kernel, (2 * width, TILE), width, zonal)

    sent = [arrived]
    for variable in range(1, variables):
        part = smooth[variable - 1].reshape(lat_count, strip, -1)
        sent.append(lax.all_to_all(part, "lat", split_axis=0, concat_axis=0, tiled=True))

    departures = []
    lines = []
    for variable in range(variables):
        mixed = meridional_forward(sent[variable], matrices, owners, groups)
        theirs = lax.ppermute(mixed[1], "obs", partner)
        departure, lifted = at_reports(
            variable, group, kept, mixed[0], theirs, ids, numbers, cells, weight, maps
        )
        departures.append(departure)
        theirs = lax.ppermute(lifted[1], "obs", partner)
        back = meridional_backward(lifted[0], theirs, matrices, groups)
        lines.append(lax.all_to_all(back, "lat", split_axis=0, concat_axis=0, tiled=True))

    gradient = None
    for variable in range(variables):
        gradient = zonal_backward(
            lines[variable].reshape(width, -1), tall, variables, variable, gradient
        )
    departure = departures[0]
    for variable in range(1, variables):
        departure = jnp.where(code >= variable * levels, departures[variable], departure)
    return (departure.reshape(report_slot.shape), gradient.reshape(control.shape))


def solution(mesh):
    in_specs = (
        P(None, "obs", "lat", None),
        P(),
        P(),
        P(),
        P(),
        P(),
        P("lat", "obs", None, None),
        P("lat", "obs", None),
        P("lat", "obs", None),
        P("lat", "obs", None, None),
        P("lat", "obs", None, None),
        P("lat", "obs", None),
        P("lat", "obs", None),
    )
    out_specs = (P("lat", "obs", None), P(None, "obs", "lat", None))
    return jax.shard_map(
        on_device, mesh=mesh, in_specs=in_specs, out_specs=out_specs, check_vma=False
    )
```
